128 devices in a mesh: row: 16 (over z_lo, y, core), col: 8 (over z_hi, x).
Axes of the slice: x: 4, y: 4, z: 4 (z_hi: 2, z_lo: 2; z = z_hi * 2 + z_lo), core: 2. Of those that a mesh axis runs over, the one named last changes fastest.
Arguments:
- features: bfloat16 [131072, 256], P(('row', 'col')), may hold values from -6 to 6
- weight: bfloat16 [256, 256], replicated, may hold values from -0.375 to 0.375
- layer_bias: float32 [256], replicated, may hold values from -3 to 3
- tile_values: bfloat16 [16, 8, 384, 128, 128], P('row', 'col'), may hold values from -0.3125 to 0.3125
- tile_rows: int32 [16, 8, 384], P('row', 'col'), may hold values from 0 to 63, as said below
- tile_cols: int32 [16, 8, 384], P('row', 'col'), may hold values from 0 to 127, as said below
- tile_count: int32 [16, 8], P('row', 'col'), may hold values from 48 to 384, as said below
- cotangent: bfloat16 [131072, 256], P(('row', 'col')), may hold values from -6 to 6
Outputs:
- activations: bfloat16 [131072, 256], P(('row', 'col'))
- grad_features: bfloat16 [131072, 256], P(('row', 'col'))
- grad_weight: float32 [256, 256], replicated
The draws below stay inside these ranges and needn't reach their ends.
Inputs may be any that keep to these rules, and one draw needn't show every extreme that they name: On each device the first tile_count slots name distinct tile positions (tile_rows, tile_cols), in increasing order of tile_cols and, within one tile column, of tile_rows; later slots hold valid but ignored positions. `tile_cols`: see tile_rows for the order of live slots. `tile_count`: live slots differ strongly from device to device; some device holds 384 in every draw.
All inputs are finite; a program needn't handle non-finite values.
Results may differ from the reference program's by a relative error of at most 0.0065.
Values may be sent and summed in bfloat16 or wider, within the bound.
No kernel may reach another device: no remote copies, remote signals or barrier semaphores. Data moves between devices by JAX's collectives and lax.ppermute only.
A program may use at most 192 MiB of HBM per device.

```python
import jax
import jax.numpy as jnp
from jax import lax

F = 256
TILE = 128
NODE_DEV = 1024
NODES = 131072
RB = 64
CB = 128
MAXT = 384
N_ROW = 16
N_COL = 8


def tile_layout(key):
    block_key, count_key, pick_key = jax.random.split(key, 3)
    device_total = N_ROW * N_COL
    positions = RB * CB
    perm_keys = jax.random.split(block_key, device_total)
    chosen = jax.vmap(lambda one_key: jax.random.permutation(one_key, positions)[:MAXT])(perm_keys)
    chosen = chosen.astype(jnp.int32)
    divisor = jax.random.randint(count_key, (device_total,), 1, 9)
    counts = (MAXT // divisor).astype(jnp.int32)
    busiest = jax.random.randint(pick_key, (), 0, device_total)
    counts = jnp.where(jnp.arange(device_total) == busiest, MAXT, counts).astype(jnp.int32)
    row_ids = chosen // CB
    col_ids = chosen % CB
    slot_ids = jnp.arange(MAXT, dtype=jnp.int32)[None, :]
    score = jnp.where(slot_ids < counts[:, None], col_ids * RB + row_ids, positions + slot_ids)
    order = jnp.argsort(score, axis=1, stable=True)
    row_ids = jnp.take_along_axis(row_ids, order, axis=1)
    col_ids = jnp.take_along_axis(col_ids, order, axis=1)
    return (row_ids.astype(jnp.int32), col_ids.astype(jnp.int32), counts)


def draw_tile_rows(key, part):
    layout = tile_layout(key)
    return layout[0].reshape(N_ROW, N_COL, MAXT)


def draw_tile_cols(key, part):
    layout = tile_layout(key)
    return layout[1].reshape(N_ROW, N_COL, MAXT)


def draw_tile_count(key, part):
    layout = tile_layout(key)
    return layout[2].reshape(N_ROW, N_COL)


def steps_of(stream_key, dims, pieces, least, top_value):
    gain, own = 1.0, jax.random.fold_in(stream_key, 6)
    for dim, shards_of in pieces:
        heights = jnp.exp(jax.random.uniform(jax.random.fold_in(own, dim), (shards_of,), jnp.float32, least / len(pieces), top_value / len(pieces)))
        gain = gain * jnp.repeat(heights, dims[dim] // shards_of).reshape([-1 if axis == dim else 1 for axis in range(len(dims))])
    return gain


def noise(stream_key, extent, scale, limit, shards=(), held_as=jnp.bfloat16):
    level = steps_of(stream_key, extent, shards, -0.22, 0.18) if shards else 1.0
    values = jax.random.normal(stream_key, extent, jnp.float32) * scale * level
    return jnp.minimum(jnp.maximum(values, -limit), limit).astype(held_as)


def setup_inputs(seed: int = 0) -> dict:
    seeds = jax.random.split(jax.random.key(seed), 9)
    return {
        "features": noise(seeds[0], (NODES, F), 1.0, 6.0, ((0, 128),)),
        "weight": noise(seeds[1], (F, F), F ** -0.5, 0.375),
        "layer_bias": noise(seeds[2], (F,), 1.0, 3.0, (), jnp.float32),
        "tile_values": noise(seeds[3], (N_ROW, N_COL, MAXT, TILE, TILE), ((N_COL * MAXT * TILE // (3 * RB)) ** -0.5), 0.3125, ((0, 16), (1, 8))),
        "tile_rows": draw_tile_rows(jax.random.fold_in(seeds[8], 71), 0),
        "tile_cols": draw_tile_cols(jax.random.fold_in(seeds[8], 71), 0),
        "tile_count": draw_tile_count(jax.random.fold_in(seeds[8], 71), 0),
        "cotangent": noise(seeds[7], (NODES, F), 1.0, 6.0, ((0, 128),)),
    }


def silu_parts(shifted):
    sig_part = jax.nn.sigmoid(shifted)
    return shifted * sig_part, sig_part * (1.0 + shifted * (1.0 - sig_part))


def reference(features, weight, layer_bias, tile_values, tile_rows, tile_cols, tile_count, cotangent):
    device_total = N_ROW * N_COL
    hidden = jnp.dot(features, weight, preferred_element_type=jnp.float32).astype(jnp.bfloat16)
    hidden_cols = hidden.reshape(N_ROW, N_COL, NODE_DEV, F).transpose(1, 0, 2, 3).reshape(N_COL, CB, TILE, F)
    all_values = tile_values.reshape(device_total, MAXT, TILE, TILE)
    all_rows = tile_rows.reshape(device_total, MAXT).astype(jnp.int32)
    all_cols = tile_cols.reshape(device_total, MAXT).astype(jnp.int32)
    all_counts = tile_count.reshape(device_total).astype(jnp.int32)
    device_ids = jnp.arange(device_total, dtype=jnp.int32)
    slot_ids = jnp.arange(MAXT, dtype=jnp.int32)

    def forward_step(totals, inputs):
        values, row_ids, col_ids, live_count, device = inputs
        row_group = device // N_COL
        col_group = device % N_COL
        live_mask = (slot_ids < live_count).astype(jnp.float32)
        selected = hidden_cols[col_group][col_ids]
        products = jnp.einsum("tij,tjf->tif", values.astype(jnp.float32), selected.astype(jnp.float32))
        products = products * live_mask[:, None, None]
        partial_value = jnp.zeros((RB, TILE, F), jnp.float32).at[row_ids].add(products)
        return totals.at[row_group].add(partial_value), None

    summed, _ = lax.scan(forward_step, jnp.zeros((N_ROW, RB, TILE, F), jnp.float32),
                         (all_values, all_rows, all_cols, all_counts, device_ids))
    aggregated = summed.reshape(NODES, F)
    shifted = aggregated + layer_bias[None, :]
    value_part, slope_part = silu_parts(shifted)
    activations = value_part.astype(jnp.bfloat16)
    grad_pre = (cotangent.astype(jnp.float32) * slope_part).astype(jnp.bfloat16)
    grad_blocks = grad_pre.reshape(N_ROW, RB, TILE, F)

    def backward_step(totals, inputs):
        values, row_ids, col_ids, live_count, device = inputs
        row_group = device // N_COL
        col_group = device % N_COL
        live_mask = (slot_ids < live_count).astype(jnp.float32)
        selected = grad_blocks[row_group][row_ids]
        products = jnp.einsum("tij,tif->tjf", values.astype(jnp.float32), selected.astype(jnp.float32))
        products = products * live_mask[:, None, None]
        partial_value = jnp.zeros((CB, TILE, F), jnp.float32).at[col_ids].add(products)
        return totals.at[col_group].add(partial_value), None

    gathered, _ = lax.scan(backward_step, jnp.zeros((N_COL, CB, TILE, F), jnp.float32),
                           (all_values, all_rows, all_cols, all_counts, device_ids))
    grad_hidden = gathered.reshape(N_COL, N_ROW, NODE_DEV, F).transpose(1, 0, 2, 3).reshape(NODES, F)
    grad_rounded = grad_hidden.astype(jnp.bfloat16)
    grad_features = lax.dot_general(grad_rounded, weight, (((1,), (1,)), ((), ())),
                                    preferred_element_type=jnp.float32).astype(jnp.bfloat16)
    grad_weight = lax.dot_general(features, grad_rounded, (((0,), (0,)), ((), ())),
                                  preferred_element_type=jnp.float32) * (NODES ** -0.5)
    return activations, grad_features, grad_weight
```

```python
import functools

import jax
import jax.numpy as jnp
from jax import lax
from jax.experimental import pallas as pl
from jax.experimental.pallas import tpu as pltpu
from jax.sharding import Mesh
from jax.sharding import PartitionSpec as P

BF16 = jnp.bfloat16
F32 = jnp.float32
ROW = ("zl", "y", "core")
COL = ("zh", "x")
VMEM_LIMIT = 58 * 2**20
PARTS = 2
BATCH = 16
CHUNK = 32


def sweep_kernel(pieces, outputs, transpose, batch, chunk, *refs):
    count, src, dst, tiles = refs[:4]
    sources = refs[4 : 4 + pieces]
    results = refs[4 + pieces : 4 + pieces + outputs]
    tile_buf, source_buf, total, tile_sems, source_sem = refs[4 + pieces + outputs :]
    size = tile_buf.shape[1]
    live = count[0]
    chunks = (live + chunk - 1) // chunk
    rows = sources[0].shape[0]

    def tile_copy(index):
        span = pl.ds(index * chunk, chunk)
        return pltpu.make_async_copy(tiles.at[span], tile_buf.at[span], tile_sems.at[index])

    def source_copy(index):
        return pltpu.make_async_copy(
            sources[index], source_buf.at[pl.ds(index * rows, rows)], source_sem.at[index]
        )

    def start_tiles(index, carry):
        tile_copy(index).start()
        return carry

    start_tiles(0, 0)
    for index in range(pieces):
        source_copy(index).start()
    lax.fori_loop(1, chunks, start_tiles, 0)
    total[...] = jnp.zeros_like(total)
    for index in range(pieces):
        source_copy(index).wait()

    contract = (((0,), (0,)), ((), ())) if transpose else (((1,), (0,)), ((), ()))

    def on_chunk(index, carry):
        tile_copy(index).wait()

        def on_batch(step, inner):
            base = index * chunk + step * batch
            products = []
            for lane in range(batch):
                start = pl.multiple_of(src[base + lane] * size, size)
                products.append(
                    lax.dot_general(
                        tile_buf[base + lane],
                        source_buf[pl.ds(start, size), :],
                        contract,
                        preferred_element_type=F32,
                    )
                )
            for lane in range(batch):
                start = pl.multiple_of(dst[base + lane] * size, size)
                span = pl.ds(start, size)
                total[span, :] = total[span, :] + products[lane]
            return inner

        steps = jnp.minimum(chunk // batch, (live - index * chunk + batch - 1) // batch)
        return lax.fori_loop(0, steps, on_batch, carry)

    lax.fori_loop(0, chunks, on_chunk, 0)
    done = 0
    for result in results:
        length = result.shape[0]
        result[...] = total[done : done + length, :].astype(result.dtype)
        done += length


def sweep(name, count, src, dst, tiles, sources, out_shapes, transpose):
    slots, size, _ = tiles.shape
    pieces = len(sources)
    rows, width = sources[0].shape
    out_rows = sum(s.shape[0] for s in out_shapes)
    chunk = min(CHUNK, slots)
    batch = min(BATCH, chunk)
    any_spec = pl.BlockSpec(memory_space=pl.ANY)
    flops = 2 * (slots // 3) * size * size * width
    return pl.pallas_call(
        functools.partial(sweep_kernel, pieces, len(out_shapes), transpose, batch, chunk),
        grid_spec=pltpu.PrefetchScalarGridSpec(
            num_scalar_prefetch=3,
            grid=(1,),
            in_specs=[any_spec] * (1 + pieces),
            out_specs=[
                pl.BlockSpec(s.shape, lambda i, *_: (0, 0), pipeline_mode=pl.Buffered(1))
                for s in out_shapes
            ],
            scratch_shapes=[
                pltpu.VMEM(tiles.shape, BF16),
                pltpu.VMEM((pieces * rows, width), BF16),
                pltpu.VMEM((out_rows + size, width), F32),
                pltpu.SemaphoreType.DMA((slots // chunk,)),
                pltpu.SemaphoreType.DMA((pieces,)),
            ],
        ),
        out_shape=out_shapes,
        compiler_params=pltpu.CompilerParams(vmem_limit_bytes=VMEM_LIMIT),
        cost_estimate=pl.CostEstimate(
            flops=flops, bytes_accessed=tiles.size * 2 + (pieces * rows + out_rows) * width * 2, transcendentals=0
        ),
        name=name,
    )(count, src, dst, tiles, *sources)


def split_dot(left, right, contract):
    high = left.astype(BF16)
    low = (left - high.astype(F32)).astype(BF16)
    first = lax.dot_general(high, right, contract, preferred_element_type=F32)
    return first + lax.dot_general(low, right, contract, preferred_element_type=F32)


def summed(refs, parts):
    per_part = len(refs) // parts
    columns = []
    for part in range(parts):
        group = refs[part * per_part : (part + 1) * per_part]
        value = group[0][...].astype(F32)
        for ref in group[1:]:
            value = value + ref[...].astype(F32)
        columns.append(value)
    return columns[0] if parts == 1 else jnp.concatenate(columns, axis=1)


def middle_kernel(parts, count, *refs):
    pieces = refs[:count]
    weight, bias, cotangent = refs[count : count + 3]
    act_ref = refs[count + 3]
    grads = refs[count + 4 : count + 4 + parts]
    weight_grad = refs[count + 4 + parts]
    gathered = summed(pieces, parts)
    shifted = split_dot(gathered, weight[...], (((1,), (0,)), ((), ()))) + bias[...]
    sig = 1.0 / (1.0 + jnp.exp(-shifted))
    act_ref[...] = (shifted * sig).astype(BF16)
    slope = sig * (1.0 + shifted * (1.0 - sig))
    grad = (cotangent[...].astype(F32) * slope).astype(BF16)
    width = grad.shape[1] // parts
    for part in range(parts):
        grads[part][...] = grad[:, part * width : (part + 1) * width]
    term = split_dot(gathered, grad, (((0,), (0,)), ((), ())))

    @pl.when(pl.program_id(0) == 0)
    def _():
        weight_grad[...] = jnp.zeros_like(weight_grad)

    weight_grad[...] += term


def middle(pieces, weight, bias, cotangent, parts):
    rows, width = cotangent.shape
    steps = 4
    block = rows // steps
    part_spec = pl.BlockSpec((block, width // parts), lambda i: (i, 0))
    wide_spec = pl.BlockSpec((block, width), lambda i: (i, 0))
    whole = pl.BlockSpec((width, width), lambda i: (0, 0))
    return pl.pallas_call(
        functools.partial(middle_kernel, parts, len(pieces)),
        grid=(steps,),
        in_specs=[part_spec] * len(pieces) + [whole, pl.BlockSpec((1, width), lambda i: (0, 0)), wide_spec],
        out_specs=[wide_spec] + [part_spec] * parts + [whole],
        out_shape=[jax.ShapeDtypeStruct((rows, width), BF16)]
        + [jax.ShapeDtypeStruct((rows, width // parts), BF16)] * parts
        + [jax.ShapeDtypeStruct((width, width), F32)],
        compiler_params=pltpu.CompilerParams(vmem_limit_bytes=VMEM_LIMIT),
        name="middle",
    )(*pieces, weight, bias.reshape(1, width), cotangent)


def final_kernel(parts, count, *refs):
    weight, out = refs[count], refs[count + 1]
    grad = summed(refs[:count], parts).astype(BF16)
    out[...] = lax.dot_general(
        grad, weight[...], (((1,), (1,)), ((), ())), preferred_element_type=F32
    ).astype(BF16)


def final(pieces, weight, parts):
    rows = pieces[0].shape[0]
    width = weight.shape[0]
    steps = 4
    block = rows // steps
    part_spec = pl.BlockSpec((block, width // parts), lambda i: (i, 0))
    return pl.pallas_call(
        functools.partial(final_kernel, parts, len(pieces)),
        grid=(steps,),
        in_specs=[part_spec] * len(pieces) + [pl.BlockSpec((width, width), lambda i: (0, 0))],
        out_specs=pl.BlockSpec((block, width), lambda i: (i, 0)),
        out_shape=jax.ShapeDtypeStruct((rows, width), BF16),
        compiler_params=pltpu.CompilerParams(vmem_limit_bytes=VMEM_LIMIT),
        name="final",
    )(*pieces, weight)


def shift(value, axes, sizes, offset):
    perm = []
    total = 1
    for size in sizes:
        total *= size
    for index in range(total):
        rest, coords = index, []
        for size in reversed(sizes):
            coords.append(rest % size)
            rest //= size
        coords.reverse()
        source = 0
        for coord, size, off in zip(coords, sizes, offset):
            source = source * size + (coord + off) % size
        perm.append((source, index))
    return lax.ppermute(value, axes, perm)


def sum_over_ring(value, axes, sizes, offsets):
    terms = [value] + [shift(value, axes, sizes, offset) for offset in offsets]
    return functools.reduce(lambda a, b: a + b, terms)


def sum_everywhere(value, core, x):
    rows = value.shape[0]
    half = rows // 2
    mine = lax.dynamic_slice_in_dim(value, core * half, half)
    other = lax.dynamic_slice_in_dim(value, (1 - core) * half, half)
    mine = mine + shift(other, "core", (2,), (1,))
    quarter = half // 4
    parts = [lax.dynamic_slice_in_dim(mine, lax.rem(x + off, 4) * quarter, quarter) for off in range(4)]
    own = parts[0]
    for off in range(1, 4):
        own = own + shift(parts[off], "x", (4,), (4 - off,))
    own = sum_over_ring(own, "y", (4,), [(1,), (2,), (3,)])
    own = sum_over_ring(own, ("zl", "zh"), (2, 2), [(0, 1), (1, 0), (1, 1)])
    ring = [own] + [shift(own, "x", (4,), (off,)) for off in range(1, 4)]
    ring = jnp.stack(ring)
    ordered = jnp.take(ring, jnp.remainder(jnp.arange(4) - x, 4), axis=0).reshape(half, -1)
    theirs = shift(ordered, "core", (2,), (1,))
    return jnp.where(core == 0, jnp.concatenate([ordered, theirs]), jnp.concatenate([theirs, ordered]))


def on_device(
    features, weight, layer_bias, tile_values, tile_rows, tile_cols, tile_count, cotangent
):
    tiles = tile_values[0, 0]
    slots, size, _ = tiles.shape
    nodes, width = features.shape
    per_slab = nodes // size
    count = tile_count.reshape(1)
    zl, y, core = (lax.axis_index(name) for name in ROW)
    zh, x = (lax.axis_index(name) for name in COL)
    rings = [(dz, dd) for dz in range(2) for dd in range(4)]
    part_width = width // PARTS

    row_ids, col_ids = tile_rows[0, 0], tile_cols[0, 0]
    row_slab, col_slab = row_ids // per_slab, col_ids // per_slab
    row_at = (((row_slab // 4) ^ zh) * 4 + (row_slab % 4 - x) % 4) * per_slab + row_ids % per_slab
    col_at = (
        (((col_slab // 8) ^ zl) * 4 + (col_slab // 2 % 4 - y) % 4) + ((col_slab % 2) ^ core) * 8
    ) * per_slab + col_ids % per_slab
    live = jnp.arange(slots, dtype=jnp.int32) < count[0]
    row_to = jnp.where(live, row_at, 8 * per_slab)
    col_to = jnp.where(live, col_at, 16 * per_slab)

    columns = [slice(part * part_width, (part + 1) * part_width) for part in range(PARTS)]
    partials = []
    for part in range(PARTS):
        own = features[:, columns[part]]
        same = [own] + [shift(own, ("zl", "y"), (2, 4), off) for off in rings[1:]]
        other = [shift(piece, "core", (2,), (1,)) for piece in same]
        partials.append(
            sweep(
                f"forward_{part}", count, col_at, row_to, tiles, same + other,
                [jax.ShapeDtypeStruct((nodes, part_width), BF16)] * 8, False,
            )
        )
    arrived = []
    for part in range(PARTS):
        arrived += [partials[part][0]]
        arrived += [
            shift(partials[part][k], COL, (2, 4), (rings[k][0], -rings[k][1])) for k in range(1, 8)
        ]
    activations, *grads, weight_term = middle(arrived, weight, layer_bias, cotangent, PARTS)

    collected = []
    for part in range(PARTS):
        own = grads[part]
        pieces = [own] + [shift(own, COL, (2, 4), off) for off in rings[1:]]
        *mine, theirs = sweep(
            f"backward_{part}", count, row_at, col_to, tiles, pieces,
            [jax.ShapeDtypeStruct((nodes, part_width), F32)] * 8
            + [jax.ShapeDtypeStruct((8 * nodes, part_width), BF16)], True,
        )
        swapped = shift(theirs, "core", (2,), (1,))
        for k in range(8):
            piece = mine[k] + swapped[k * nodes : (k + 1) * nodes].astype(F32)
            piece = piece.astype(BF16)
            if k:
                piece = shift(piece, ("zl", "y"), (2, 4), (rings[k][0], -rings[k][1]))
            collected.append(piece)
    grad_features = final(collected, weight, PARTS)
    grad_weight = sum_everywhere(weight_term, core, x)
    total_nodes = nodes * 128
    return activations, grad_features, grad_weight * float(total_nodes) ** -0.5


def solution(mesh):
    fine = Mesh(mesh.devices.reshape(2, 4, 2, 2, 4), ROW + COL)
    nodes = P(ROW + COL, None)
    return jax.shard_map(
        on_device,
        mesh=fine,
        in_specs=(
            nodes,
            P(),
            P(),
            P(ROW, COL, None, None, None),
            P(ROW, COL, None),
            P(ROW, COL, None),
            P(ROW, COL),
            nodes,
        ),
        out_specs=(nodes, nodes, P()),
        check_vma=False,
    )
```

```python
import functools

import jax
import jax.numpy as jnp
from jax import lax
from jax.experimental import pallas as pl
from jax.experimental.pallas import tpu as pltpu
from jax.sharding import Mesh
from jax.sharding import PartitionSpec as P

BF16 = jnp.bfloat16
F32 = jnp.float32
ROW = ("zl", "y", "core")
COL = ("zh", "x")
VMEM_LIMIT = 58 * 2**20
PARTS = 2
BATCH = 16
CHUNK = 32


def sweep_kernel(plan, transpose, batch, chunk, *refs):
    source_plan, result_plan, slab = plan
    pieces, outputs = len(source_plan), len(result_plan)
    count, src, dst, tiles = refs[:4]
    sources = refs[4 : 4 + pieces]
    results = refs[4 + pieces : 4 + pieces + outputs]
    tile_buf, source_buf, total, tile_sems, source_sem = refs[4 + pieces + outputs :]
    size = tile_buf.shape[1]
    live = count[0]
    chunks = (live + chunk - 1) // chunk

    def tile_copy(index):
        span = pl.ds(index * chunk, chunk)
        return pltpu.make_async_copy(tiles.at[span], tile_buf.at[span], tile_sems.at[index])

    source_copies = []
    for source, places in zip(sources, source_plan):
        for offset, place, slabs, column in places:
            source_copies.append(
                pltpu.make_async_copy(
                    source.at[pl.ds(offset * slab, slabs * slab)],
                    source_buf.at[pl.ds(place * slab, slabs * slab), pl.ds(column, source.shape[1])],
                    source_sem.at[len(source_copies)],
                )
            )

    def start_tiles(index, carry):
        tile_copy(index).start()
        return carry

    start_tiles(0, 0)
    for copy in source_copies:
        copy.start()
    lax.fori_loop(1, chunks, start_tiles, 0)
    total[...] = jnp.zeros_like(total)
    for copy in source_copies:
        copy.wait()

    contract = (((0,), (0,)), ((), ())) if transpose else (((1,), (0,)), ((), ()))

    def on_chunk(index, carry):
        tile_copy(index).wait()

        def on_batch(step, inner):
            base = index * chunk + step * batch
            products = []
            for lane in range(batch):
                start = pl.multiple_of(src[base + lane] * size, size)
                products.append(
                    lax.dot_general(
                        tile_buf[base + lane],
                        source_buf[pl.ds(start, size), :],
                        contract,
                        preferred_element_type=F32,
                    )
                )
            for lane in range(batch):
                start = pl.multiple_of(dst[base + lane] * size, size)
                span = pl.ds(start, size)
                total[span, :] = total[span, :] + products[lane]
            return inner

        steps = jnp.minimum(chunk // batch, (live - index * chunk + batch - 1) // batch)
        return lax.fori_loop(0, steps, on_batch, carry)

    lax.fori_loop(0, chunks, on_chunk, 0)
    for result, (slabs, column) in zip(results, result_plan):
        for index, place in enumerate(slabs):
            result[index * slab : (index + 1) * slab, :] = total[
                place * slab : (place + 1) * slab, column : column + result.shape[1]
            ].astype(result.dtype)


def sweep(name, count, src, dst, tiles, sources, source_plan, result_plan, result_types, slab, width, transpose):
    slots, size, _ = tiles.shape
    part_width = width // PARTS
    source_slabs = max(p + n for places in source_plan for _, p, n, _ in places)
    result_slabs = max(max(slabs) for slabs, _ in result_plan) + 1
    copies = sum(len(places) for places in source_plan)
    chunk = min(CHUNK, slots)
    batch = min(BATCH, chunk)
    any_spec = pl.BlockSpec(memory_space=pl.ANY)
    out_shapes = [
        jax.ShapeDtypeStruct((len(slabs) * slab, part_width), kind)
        for (slabs, _), kind in zip(result_plan, result_types)
    ]
    moved, flops = 1024, 1024
    return pl.pallas_call(
        functools.partial(sweep_kernel, (source_plan, result_plan, slab), transpose, batch, chunk),
        grid_spec=pltpu.PrefetchScalarGridSpec(
            num_scalar_prefetch=3,
            grid=(1,),
            in_specs=[any_spec] * (1 + len(sources)),
            out_specs=[
                pl.BlockSpec(s.shape, lambda i, *_: (0, 0), pipeline_mode=pl.Buffered(1))
                for s in out_shapes
            ],
            scratch_shapes=[
                pltpu.VMEM(tiles.shape, BF16),
                pltpu.VMEM((source_slabs * slab, width), BF16),
                pltpu.VMEM((result_slabs * slab + size, width), F32),
                pltpu.SemaphoreType.DMA((slots // chunk,)),
                pltpu.SemaphoreType.DMA((copies,)),
            ],
        ),
        out_shape=out_shapes,
        compiler_params=pltpu.CompilerParams(vmem_limit_bytes=VMEM_LIMIT),
        cost_estimate=pl.CostEstimate(
            flops=flops, bytes_accessed=moved, transcendentals=0
        ),
        name=name,
    )(count, src, dst, tiles, *sources)


def split_dot(left, right, contract):
    high = left.astype(BF16)
    low = (left - high.astype(F32)).astype(BF16)
    first = lax.dot_general(high, right, contract, preferred_element_type=F32)
    return first + lax.dot_general(low, right, contract, preferred_element_type=F32)


def summed(refs, parts):
    per_part = len(refs) // parts
    columns = []
    for part in range(parts):
        group = refs[part * per_part : (part + 1) * per_part]
        value = group[0][...].astype(F32)
        for ref in group[1:]:
            value = value + ref[...].astype(F32)
        columns.append(value)
    return columns[0] if parts == 1 else jnp.concatenate(columns, axis=1)


def middle_kernel(parts, count, *refs):
    pieces = refs[:count]
    weight, bias, cotangent = refs[count : count + 3]
    act_ref = refs[count + 3]
    grads = refs[count + 4 : count + 4 + parts]
    weight_grad = refs[count + 4 + parts]
    gathered = summed(pieces, parts)
    shifted = split_dot(gathered, weight[...], (((1,), (0,)), ((), ()))) + bias[...]
    sig = 1.0 / (1.0 + jnp.exp(-shifted))
    act_ref[...] = (shifted * sig).astype(BF16)
    slope = sig * (1.0 + shifted * (1.0 - sig))
    grad = (cotangent[...].astype(F32) * slope).astype(BF16)
    width = grad.shape[1] // parts
    for part in range(parts):
        grads[part][...] = grad[:, part * width : (part + 1) * width]
    term = split_dot(gathered, grad, (((0,), (0,)), ((), ())))

    @pl.when(pl.program_id(0) == 0)
    def _():
        weight_grad[...] = jnp.zeros_like(weight_grad)

    weight_grad[...] += term


def middle(pieces, weight, bias, cotangent, parts):
    rows, width = cotangent.shape
    steps = 4
    block = rows // steps
    part_spec = pl.BlockSpec((block, width // parts), lambda i: (i, 0))
    wide_spec = pl.BlockSpec((block, width), lambda i: (i, 0))
    whole = pl.BlockSpec((width, width), lambda i: (0, 0))
    return pl.pallas_call(
        functools.partial(middle_kernel, parts, len(pieces)),
        grid=(steps,),
        in_specs=[part_spec] * len(pieces) + [whole, pl.BlockSpec((1, width), lambda i: (0, 0)), wide_spec],
        out_specs=[wide_spec] + [part_spec] * parts + [whole],
        out_shape=[jax.ShapeDtypeStruct((rows, width), BF16)]
        + [jax.ShapeDtypeStruct((rows, width // parts), BF16)] * parts
        + [jax.ShapeDtypeStruct((width, width), F32)],
        compiler_params=pltpu.CompilerParams(vmem_limit_bytes=VMEM_LIMIT),
        name="middle",
    )(*pieces, weight, bias.reshape(1, width), cotangent)


def final_kernel(parts, count, *refs):
    weight, out = refs[count], refs[count + 1]
    grad = summed(refs[:count], parts).astype(BF16)
    out[...] = lax.dot_general(
        grad, weight[...], (((1,), (1,)), ((), ())), preferred_element_type=F32
    ).astype(BF16)


def final(pieces, weight, parts):
    rows = pieces[-1].shape[0]
    width = weight.shape[0]
    steps = 4
    block = rows // steps
    part_spec = pl.BlockSpec((block, width // parts), lambda i: (i, 0))
    return pl.pallas_call(
        functools.partial(final_kernel, parts, len(pieces)),
        grid=(steps,),
        in_specs=[part_spec] * len(pieces) + [pl.BlockSpec((width, width), lambda i: (0, 0))],
        out_specs=pl.BlockSpec((block, width), lambda i: (i, 0)),
        out_shape=jax.ShapeDtypeStruct((rows, width), BF16),
        compiler_params=pltpu.CompilerParams(vmem_limit_bytes=VMEM_LIMIT),
        name="final",
    )(*pieces, weight)


def shift(value, axes, sizes, offset):
    perm = []
    total = 1
    for size in sizes:
        total *= size
    for index in range(total):
        rest, coords = index, []
        for size in reversed(sizes):
            coords.append(rest % size)
            rest //= size
        coords.reverse()
        source = 0
        for coord, size, off in zip(coords, sizes, offset):
            source = source * size + (coord + off) % size
        perm.append((source, index))
    return lax.ppermute(value, axes, perm)


def add(*terms):
    return functools.reduce(lambda a, b: a + b, [term.astype(F32) for term in terms])


def toward(value, axes, dz, dr):
    return shift(value, axes, (2, 4), (dz, -dr))


def scatter_ring_first(held, axes):
    nodes = held[0].shape[0] // 2
    arrived = [held[0]] + [toward(held[dr], axes, 0, dr) for dr in range(1, 4)]
    other = add(*[piece[nodes:] for piece in arrived]).astype(BF16)
    return arrived + [toward(other, axes, 1, 0)]


def scatter_pair_first(held, axes):
    nodes = held[0].shape[0] // 4
    arrived = [held[0], toward(held[1], axes, 1, 0)]
    terms = []
    for dr in range(1, 4):
        span = slice(dr * nodes, (dr + 1) * nodes)
        terms.append(toward(add(arrived[0][span], arrived[1][span]).astype(BF16), axes, 0, dr))
    return arrived + terms


def join_kernel(first, first_pair, *refs):
    ring, terms = refs[:4], refs[4:8]
    pair, both, total = refs[8:]
    nodes = first.shape[0]
    pair[:nodes, :] = first[...]
    pair[nodes:, :] = first_pair[...]
    for index, piece in enumerate(ring):
        both[index * nodes : (index + 1) * nodes, :] = piece[...]
    total[...] = (terms[0][...] + terms[1][...]) + (terms[2][...] + terms[3][...])


def join(first, first_pair, ring, terms):
    nodes, width = first.shape
    return pl.pallas_call(
        join_kernel,
        out_shape=[
            jax.ShapeDtypeStruct((2 * nodes, width), BF16),
            jax.ShapeDtypeStruct((4 * nodes, width), BF16),
            jax.ShapeDtypeStruct(terms[0].shape, F32),
        ],
        compiler_params=pltpu.CompilerParams(vmem_limit_bytes=VMEM_LIMIT),
        cost_estimate=pl.CostEstimate(flops=1024, bytes_accessed=1024, transcendentals=0),
        name="join",
    )(first, first_pair, *ring, *terms)


def around(value, axes, sizes, offsets):
    return [value] + [shift(value, axes, sizes, offset) for offset in offsets]


RING_FIRST = [[dr, 4 + dr] for dr in range(4)]
PAIR_FIRST = [[0, 1, 2, 3], [4, 5, 6, 7]]
GATHERED_PAIR_FIRST = [[(0, dr, 1), (1, 4 + dr, 1)] for dr in range(4)]
GATHERED_RING_FIRST = [[(0, dr, 1)] for dr in range(4)] + [[(0, 4, 4)]]


def at_column(plan, column):
    return [[(*place, column) for place in places] for places in plan]


def on_device(
    features, weight, layer_bias, tile_values, tile_rows, tile_cols, tile_count, cotangent
):
    tiles = tile_values[0, 0]
    slots, size, _ = tiles.shape
    nodes, width = features.shape
    per_slab = nodes // size
    count = tile_count.reshape(1)
    zl, y, core = (lax.axis_index(name) for name in ROW)
    zh, x = (lax.axis_index(name) for name in COL)
    part_width = width // PARTS
    row_axes, col_axes = ("zl", "y"), ("zh", "x")

    row_ids, col_ids = tile_rows[0, 0], tile_cols[0, 0]
    row_slab, col_slab = row_ids // per_slab, col_ids // per_slab
    row_at = (((row_slab // 4) ^ zh) * 4 + (row_slab % 4 - x) % 4) * per_slab + row_ids % per_slab
    col_at = (
        (((col_slab // 8) ^ zl) * 4 + (col_slab // 2 % 4 - y) % 4) + ((col_slab % 2) ^ core) * 8
    ) * per_slab + col_ids % per_slab
    live = jnp.arange(slots, dtype=jnp.int32) < count[0]
    row_to = jnp.where(live, row_at, 8 * per_slab)
    col_to = jnp.where(live, col_at, 16 * per_slab)

    whole = lax.all_gather(features, ROW, axis=0, tiled=True)
    plan = [(slabs, 0) for slabs in RING_FIRST] + [(slabs, part_width) for slabs in PAIR_FIRST]
    held = sweep(
        "forward", count, col_ids, row_to, tiles, [whole], [[(0, 0, 16, 0)]],
        plan, [BF16] * len(plan), nodes, width, False,
    )
    arrived = scatter_ring_first(held[:4], col_axes) + scatter_pair_first(held[4:], col_axes)
    activations, first, second, weight_term = middle(arrived, weight, layer_bias, cotangent, PARTS)

    ring_steps = [(0, 1), (0, 2), (0, 3)]
    first_pair = shift(first, col_axes, (2, 4), (1, 0))
    ring = around(second, col_axes, (2, 4), ring_steps)
    terms = around(weight_term, row_axes, (2, 4), ring_steps)
    pair, both, weight_sum = join(first, first_pair, ring, terms)
    gathered = around(pair, col_axes, (2, 4), ring_steps) + ring
    gathered.append(shift(both, col_axes, (2, 4), (1, 0)))
    weight_sum = add(*around(weight_sum, "core", (2,), [(1,)]))

    order = [[slab for slabs in plan for slab in slabs] for plan in (RING_FIRST, PAIR_FIRST)]
    results = sweep(
        "backward", count, row_at, col_to, tiles, gathered + [weight_sum],
        at_column(GATHERED_PAIR_FIRST, 0) + at_column(GATHERED_RING_FIRST, part_width) + [[]],
        [(slabs, part * part_width) for part, slabs in enumerate(order)]
        + [([8 + slab for slab in slabs], part * part_width) for part, slabs in enumerate(order)],
        [F32, F32, BF16, BF16], nodes, width, True,
    )
    collected = []
    for part, plan in enumerate((RING_FIRST, PAIR_FIRST)):
        mine, theirs = results[part], results[2 + part]
        swapped = shift(theirs, "core", (2,), (1,))
        held, done = [], 0
        for slabs in plan:
            span = slice(done * nodes, (done + len(slabs)) * nodes)
            held.append(add(mine[span], swapped[span]).astype(BF16))
            done += len(slabs)
        scatter = scatter_ring_first if part == 0 else scatter_pair_first
        collected += scatter(held, row_axes)
    grad_features = final(collected, weight, PARTS)
    weight_sum = add(*around(weight_sum, "x", (4,), [(1,), (2,), (3,)]))
    grad_weight = add(*around(weight_sum, ("zl", "zh"), (2, 2), [(0, 1), (1, 0), (1, 1)]))
    total_nodes = nodes * 128
    return activations, grad_features, grad_weight * float(total_nodes) ** -0.5


def solution(mesh):
    fine = Mesh(mesh.devices.reshape(2, 4, 2, 2, 4), ROW + COL)
    nodes = P(ROW + COL, None)
    return jax.shard_map(
        on_device,
        mesh=fine,
        in_specs=(
            nodes,
            P(),
            P(),
            P(ROW, COL, None, None, None),
            P(ROW, COL, None),
            P(ROW, COL, None),
            P(ROW, COL),
            nodes,
        ),
        out_specs=(nodes, nodes, P()),
        check_vma=False,
    )
```

```python
import functools

import jax
import jax.numpy as jnp
from jax import lax
from jax.experimental import pallas as pl
from jax.experimental.pallas import tpu as pltpu
from jax.sharding import Mesh
from jax.sharding import PartitionSpec as P

BF16 = jnp.bfloat16
F32 = jnp.float32
ROW = ("zl", "y", "core")
COL = ("zh", "x")
VMEM_LIMIT = 58 * 2**20
PARTS = 2
BATCH = 48
CHUNK = 48


def accumulate(source_buf, tile_buf, total, src, dst, contract, batch, base):
    size = tile_buf.shape[1]
    products = []
    for lane in range(batch):
        start = pl.multiple_of(src[base + lane] * size, size)
        products.append(
            lax.dot_general(
                tile_buf[base + lane],
                source_buf[pl.ds(start, size), :],
                contract,
                preferred_element_type=F32,
            )
        )
    for lane in range(batch):
        span = pl.ds(pl.multiple_of(dst[base + lane] * size, size), size)
        total[span, :] = total[span, :] + products[lane]


def source_copies_of(sources, source_plan, source_buf, source_sems, slab):
    half = source_buf.shape[1] // PARTS
    copies = []
    for source, places in zip(sources, source_plan):
        for offset, place, number, part in places:
            copies.append(
                pltpu.make_async_copy(
                    source.at[pl.ds(offset * slab, number * slab)],
                    source_buf.at[pl.ds(place * slab, number * slab), pl.ds(part * half, half)],
                    source_sems.at[len(copies)],
                )
            )
    return copies


def forward_kernel(source_plan, result_plan, slab, batch, chunk, *refs):
    pieces, outputs = len(source_plan), len(result_plan)
    count, src, dst, tiles = refs[:4]
    sources = refs[4 : 4 + pieces]
    results = refs[4 + pieces : 4 + pieces + outputs]
    tile_buf, source_buf, total, stage, tile_sems, source_sems, result_sems = refs[4 + pieces + outputs :]
    live = count[0]
    chunks = (live + chunk - 1) // chunk

    def tile_copy(index):
        span = pl.ds(index * chunk, chunk)
        return pltpu.make_async_copy(tiles.at[span], tile_buf.at[span], tile_sems.at[index])

    source_copies = source_copies_of(sources, source_plan, source_buf, source_sems, slab)

    def start_tiles(index, carry):
        tile_copy(index).start()
        return carry

    start_tiles(0, 0)
    for copy in source_copies:
        copy.start()
    lax.fori_loop(1, chunks, start_tiles, 0)
    total[...] = jnp.zeros_like(total)
    for copy in source_copies:
        copy.wait()

    def on_chunk(index, carry):
        tile_copy(index).wait()

        def on_batch(step, inner):
            base = index * chunk + step * batch
            accumulate(
                source_buf, tile_buf, total, src, dst, (((1,), (0,)), ((), ())), batch, base
            )
            return inner

        steps = jnp.minimum(chunk // batch, (live - index * chunk + batch - 1) // batch)
        return lax.fori_loop(0, steps, on_batch, carry)

    lax.fori_loop(0, chunks, on_chunk, 0)
    copies = []
    for place in range(stage.shape[0] // slab):
        rows = slice(place * slab, (place + 1) * slab)
        stage[rows, :] = total[rows, :].astype(BF16)
        for result, (held, column) in zip(results, result_plan):
            if place in held:
                copy = pltpu.make_async_copy(
                    stage.at[pl.ds(place * slab, slab), pl.ds(column, result.shape[1])],
                    result.at[pl.ds(held.index(place) * slab, slab)],
                    result_sems.at[len(copies)],
                )
                copy.start()
                copies.append(copy)
    for copy in copies:
        copy.wait()


def forward_sweep(count, src, dst, tiles, sources, source_plan, result_plan, slab, width):
    slots, size, _ = tiles.shape
    part_width = width // PARTS
    source_slabs = max(p + n for places in source_plan for _, p, n, _ in places)
    source_copies = sum(len(places) for places in source_plan)
    result_slabs = max(max(slabs) for slabs, _ in result_plan) + 1
    copies = sum(len(slabs) for slabs, _ in result_plan)
    chunk = min(CHUNK, slots)
    batch = min(BATCH, chunk)
    any_spec = pl.BlockSpec(memory_space=pl.ANY)
    return pl.pallas_call(
        functools.partial(forward_kernel, source_plan, result_plan, slab, batch, chunk),
        grid_spec=pltpu.PrefetchScalarGridSpec(
            num_scalar_prefetch=3,
            grid=(1,),
            in_specs=[any_spec] * (1 + len(sources)),
            out_specs=[any_spec] * len(result_plan),
            scratch_shapes=[
                pltpu.VMEM(tiles.shape, BF16),
                pltpu.VMEM((source_slabs * slab, width), BF16),
                pltpu.VMEM((result_slabs * slab + size, width), F32),
                pltpu.VMEM((result_slabs * slab, width), BF16),
                pltpu.SemaphoreType.DMA((slots // chunk,)),
                pltpu.SemaphoreType.DMA((source_copies,)),
                pltpu.SemaphoreType.DMA((copies,)),
            ],
        ),
        out_shape=[
            jax.ShapeDtypeStruct((len(slabs) * slab, part_width), BF16) for slabs, _ in result_plan
        ],
        compiler_params=pltpu.CompilerParams(vmem_limit_bytes=VMEM_LIMIT),
        cost_estimate=pl.CostEstimate(flops=1024, bytes_accessed=1024, transcendentals=0),
        name="forward",
    )(count, src, dst, tiles, *sources)


def backward_kernel(source_plan, slab, batch, chunk, *refs):
    pieces = len(source_plan)
    count, src, dst, slab_at, tiles = refs[:5]
    sources = refs[5 : 5 + pieces]
    results = refs[5 + pieces : 9 + pieces]
    tile_buf, source_buf, total, stage, tile_sems, source_sems, result_sems = refs[9 + pieces :]
    live = count[0]
    chunks = (live + chunk - 1) // chunk
    slabs = stage.shape[0] // slab
    per_slab = slab // tile_buf.shape[1]
    half = results[0].shape[1]

    def tile_copy(index):
        span = pl.ds(index * chunk, chunk)
        return pltpu.make_async_copy(tiles.at[span], tile_buf.at[span], tile_sems.at[index])

    source_copies = source_copies_of(sources, source_plan, source_buf, source_sems, slab)

    def start_tiles(index, carry):
        tile_copy(index).start()
        return carry

    start_tiles(0, 0)
    for copy in source_copies:
        copy.start()
    lax.fori_loop(1, chunks, start_tiles, 0)
    total[...] = jnp.zeros_like(total)
    for copy in source_copies:
        copy.wait()

    def result_copy(result, place, at, part):
        return pltpu.make_async_copy(
            stage.at[pl.ds(pl.multiple_of(place * slab, slab), slab), pl.ds(part * half, half)],
            result.at[pl.ds(pl.multiple_of(at * slab, slab), slab)],
            result_sems.at[place, part],
        )

    def flush(place, carry):
        rows = pl.ds(pl.multiple_of(place * slab, slab), slab)
        stage[rows, :] = total[rows, :].astype(BF16)
        offset = slab_at[place]
        at = offset % 8
        ring_at = (at % 4) * 2 + at // 4

        @pl.when(offset < 8)
        def _():
            result_copy(results[0], place, ring_at, 0).start()
            result_copy(results[1], place, at, 1).start()

        @pl.when(offset >= 8)
        def _():
            result_copy(results[2], place, ring_at, 0).start()
            result_copy(results[3], place, at, 1).start()

        return carry

    def on_chunk(index, flushed):
        tile_copy(index).wait()

        def on_batch(step, inner):
            base = index * chunk + step * batch
            accumulate(
                source_buf, tile_buf, total, src, dst, (((0,), (0,)), ((), ())), batch, base
            )
            return inner

        steps = jnp.minimum(chunk // batch, (live - index * chunk + batch - 1) // batch)
        lax.fori_loop(0, steps, on_batch, 0)
        last = jnp.minimum((index + 1) * chunk, live) - 1
        ready = jnp.where(index + 1 == chunks, slabs, dst[last] // per_slab)
        lax.fori_loop(flushed, ready, flush, 0)
        return ready

    lax.fori_loop(0, chunks, on_chunk, 0)
    for place in range(slabs):
        for part in range(2):
            result_copy(results[part], place, 0, part).wait()


def backward_sweep(count, src, dst, slab_at, tiles, sources, source_plan, slab, width):
    slots, size, _ = tiles.shape
    part_width = width // PARTS
    source_slabs = max(p + n for places in source_plan for _, p, n, _ in places)
    slabs = slab_at.shape[0]
    copies = sum(len(places) for places in source_plan)
    chunk = min(CHUNK, slots)
    batch = min(BATCH, chunk)
    any_spec = pl.BlockSpec(memory_space=pl.ANY)
    return pl.pallas_call(
        functools.partial(backward_kernel, source_plan, slab, batch, chunk),
        grid_spec=pltpu.PrefetchScalarGridSpec(
            num_scalar_prefetch=4,
            grid=(1,),
            in_specs=[any_spec] * (1 + len(sources)),
            out_specs=[any_spec] * 4,
            scratch_shapes=[
                pltpu.VMEM(tiles.shape, BF16),
                pltpu.VMEM((source_slabs * slab, width), BF16),
                pltpu.VMEM((slabs * slab + size, width), F32),
                pltpu.VMEM((slabs * slab, width), BF16),
                pltpu.SemaphoreType.DMA((slots // chunk,)),
                pltpu.SemaphoreType.DMA((copies,)),
                pltpu.SemaphoreType.DMA((slabs, 2)),
            ],
        ),
        out_shape=[jax.ShapeDtypeStruct((slabs // 2 * slab, part_width), BF16)] * 4,
        compiler_params=pltpu.CompilerParams(vmem_limit_bytes=VMEM_LIMIT),
        cost_estimate=pl.CostEstimate(flops=1024, bytes_accessed=1024, transcendentals=0),
        name="backward",
    )(count, src, dst, slab_at, tiles, *sources)


def split_dot(left, right, contract):
    high = left.astype(BF16)
    low = (left - high.astype(F32)).astype(BF16)
    first = lax.dot_general(high, right, contract, preferred_element_type=F32)
    return first + lax.dot_general(low, right, contract, preferred_element_type=F32)


def summed(refs, parts):
    per_part = len(refs) // parts
    columns = []
    for part in range(parts):
        group = refs[part * per_part : (part + 1) * per_part]
        value = group[0][...].astype(F32)
        for ref in group[1:]:
            value = value + ref[...].astype(F32)
        columns.append(value)
    return columns[0] if parts == 1 else jnp.concatenate(columns, axis=1)


def middle_kernel(parts, count, *refs):
    pieces = refs[:count]
    weight, bias, cotangent = refs[count : count + 3]
    act_ref = refs[count + 3]
    grads = refs[count + 4 : count + 4 + parts]
    weight_grad = refs[count + 4 + parts]
    gathered = summed(pieces, parts)
    shifted = split_dot(gathered, weight[...], (((1,), (0,)), ((), ()))) + bias[...]
    sig = 1.0 / (1.0 + jnp.exp(-shifted))
    act_ref[...] = (shifted * sig).astype(BF16)
    slope = sig * (1.0 + shifted * (1.0 - sig))
    grad = (cotangent[...].astype(F32) * slope).astype(BF16)
    width = grad.shape[1] // parts
    for part in range(parts):
        grads[part][...] = grad[:, part * width : (part + 1) * width]
    term = lax.dot_general(
        gathered.astype(BF16), grad, (((0,), (0,)), ((), ())), preferred_element_type=F32
    )

    @pl.when(pl.program_id(0) == 0)
    def _():
        weight_grad[...] = jnp.zeros_like(weight_grad)

    weight_grad[...] += term


def middle(pieces, weight, bias, cotangent, parts):
    rows, width = cotangent.shape
    steps = 4
    block = rows // steps
    part_spec = pl.BlockSpec((block, width // parts), lambda i: (i, 0))
    wide_spec = pl.BlockSpec((block, width), lambda i: (i, 0))
    whole = pl.BlockSpec((width, width), lambda i: (0, 0))
    return pl.pallas_call(
        functools.partial(middle_kernel, parts, len(pieces)),
        grid=(steps,),
        in_specs=[part_spec] * len(pieces) + [whole, pl.BlockSpec((1, width), lambda i: (0, 0)), wide_spec],
        out_specs=[wide_spec] + [part_spec] * parts + [whole],
        out_shape=[jax.ShapeDtypeStruct((rows, width), BF16)]
        + [jax.ShapeDtypeStruct((rows, width // parts), BF16)] * parts
        + [jax.ShapeDtypeStruct((width, width), F32)],
        compiler_params=pltpu.CompilerParams(vmem_limit_bytes=VMEM_LIMIT),
        name="middle",
    )(*pieces, weight, bias.reshape(1, width), cotangent)


def final_kernel(parts, count, *refs):
    weight, out = refs[count], refs[count + 1]
    grad = summed(refs[:count], parts).astype(BF16)
    out[...] = lax.dot_general(
        grad, weight[...], (((1,), (1,)), ((), ())), preferred_element_type=F32
    ).astype(BF16)


def final(pieces, weight, parts):
    rows = pieces[-1].shape[0]
    width = weight.shape[0]
    steps = 4
    block = rows // steps
    part_spec = pl.BlockSpec((block, width // parts), lambda i: (i, 0))
    return pl.pallas_call(
        functools.partial(final_kernel, parts, len(pieces)),
        grid=(steps,),
        in_specs=[part_spec] * len(pieces) + [pl.BlockSpec((width, width), lambda i: (0, 0))],
        out_specs=pl.BlockSpec((block, width), lambda i: (i, 0)),
        out_shape=jax.ShapeDtypeStruct((rows, width), BF16),
        compiler_params=pltpu.CompilerParams(vmem_limit_bytes=VMEM_LIMIT),
        name="final",
    )(*pieces, weight)


def shift(value, axes, sizes, offset):
    perm = []
    total = 1
    for size in sizes:
        total *= size
    for index in range(total):
        rest, coords = index, []
        for size in reversed(sizes):
            coords.append(rest % size)
            rest //= size
        coords.reverse()
        source = 0
        for coord, size, off in zip(coords, sizes, offset):
            source = source * size + (coord + off) % size
        perm.append((source, index))
    return lax.ppermute(value, axes, perm)


def add(*terms):
    return functools.reduce(lambda a, b: a + b, [term.astype(F32) for term in terms])


def toward(value, axes, dz, dr):
    return shift(value, axes, (2, 4), (dz, -dr))


def scatter_ring_first(held, axes):
    nodes = held[0].shape[0] // 2
    arrived = [held[0]] + [toward(held[dr], axes, 0, dr) for dr in range(1, 4)]
    other = add(*[piece[nodes:] for piece in arrived]).astype(BF16)
    return arrived + [toward(other, axes, 1, 0)]


def scatter_pair_first(held, axes):
    nodes = held[0].shape[0] // 4
    arrived = [held[0], toward(held[1], axes, 1, 0)]
    terms = []
    for dr in range(1, 4):
        span = slice(dr * nodes, (dr + 1) * nodes)
        terms.append(toward(add(arrived[0][span], arrived[1][span]).astype(BF16), axes, 0, dr))
    return arrived + terms


def join_kernel(first, first_pair, *refs):
    ring = refs[:4]
    pair, both = refs[4:]
    nodes = first.shape[0]
    pair[:nodes, :] = first[...]
    pair[nodes:, :] = first_pair[...]
    for index, piece in enumerate(ring):
        both[index * nodes : (index + 1) * nodes, :] = piece[...]


def join(first, first_pair, ring):
    nodes, width = first.shape
    return pl.pallas_call(
        join_kernel,
        out_shape=[
            jax.ShapeDtypeStruct((2 * nodes, width), BF16),
            jax.ShapeDtypeStruct((4 * nodes, width), BF16),
        ],
        compiler_params=pltpu.CompilerParams(vmem_limit_bytes=VMEM_LIMIT),
        cost_estimate=pl.CostEstimate(flops=1024, bytes_accessed=1024, transcendentals=0),
        name="join",
    )(first, first_pair, *ring)


def around(value, axes, sizes, offsets):
    return [value] + [shift(value, axes, sizes, offset) for offset in offsets]


def gather(first, second, axes):
    ring_steps = [(0, 1), (0, 2), (0, 3)]
    first_pair = shift(first, axes, (2, 4), (1, 0))
    ring = around(second, axes, (2, 4), ring_steps)
    pair, both = join(first, first_pair, ring)
    later = [shift(pair, axes, (2, 4), step) for step in ring_steps]
    return [pair, both], later + [shift(both, axes, (2, 4), (1, 0))]


RING_FIRST = [[dr, 4 + dr] for dr in range(4)]
PAIR_FIRST = [[0, 1, 2, 3], [4, 5, 6, 7]]
GATHERED = [
    [(0, 0, 1, 0), (1, 4, 1, 0)],
    [(0, 0, 4, 1)],
    *[[(0, dr, 1, 0), (1, 4 + dr, 1, 0)] for dr in range(1, 4)],
    [(0, 4, 4, 1)],
]
OTHER_CORE = [[(at, held + 8, slabs, half) for at, held, slabs, half in places] for places in GATHERED]


def on_device(
    features, weight, layer_bias, tile_values, tile_rows, tile_cols, tile_count, cotangent
):
    tiles = tile_values[0, 0]
    slots, size, _ = tiles.shape
    nodes, width = features.shape
    per_slab = nodes // size
    count = tile_count.reshape(1)
    zl, y, core = (lax.axis_index(name) for name in ROW)
    zh, x = (lax.axis_index(name) for name in COL)
    part_width = width // PARTS
    row_axes, col_axes = ("zl", "y"), ("zh", "x")

    row_ids, col_ids = tile_rows[0, 0], tile_cols[0, 0]
    row_slab = row_ids // per_slab
    row_at = (((row_slab // 4) ^ zh) * 4 + (row_slab % 4 - x) % 4) * per_slab + row_ids % per_slab
    every = jnp.arange(16, dtype=jnp.int32)
    slab_at = (((every // 8) ^ zl) * 4 + (every // 2 % 4 - y) % 4) + ((every % 2) ^ core) * 8
    live = jnp.arange(slots, dtype=jnp.int32) < count[0]
    row_to = jnp.where(live, row_at, 8 * per_slab)
    col_slab = col_ids // per_slab
    col_from = (
        (((col_slab // 8) ^ zl) * 4 + (col_slab // 2 % 4 - y) % 4) + ((col_slab % 2) ^ core) * 8
    ) * per_slab + col_ids % per_slab
    col_to = jnp.where(live, col_ids, 16 * per_slab)

    early, later = gather(features[:, :part_width], features[:, part_width:], row_axes)
    others = [shift(piece, "core", (2,), (1,)) for piece in early + later]
    plan = [(slabs, 0) for slabs in RING_FIRST] + [(slabs, part_width) for slabs in PAIR_FIRST]
    held = forward_sweep(
        count, col_from, row_to, tiles, early + later + others, GATHERED + OTHER_CORE, plan, nodes, width
    )
    arrived = scatter_ring_first(held[:4], col_axes) + scatter_pair_first(held[4:], col_axes)
    activations, first, second, weight_term = middle(arrived, weight, layer_bias, cotangent, PARTS)

    early, later = gather(first, second, col_axes)
    weight_sum = add(*around(weight_term, row_axes, (2, 4), [(0, 1), (0, 2), (0, 3)]))
    results = backward_sweep(
        count, row_at, col_to, slab_at, tiles, early + later + [weight_sum], GATHERED + [[]], nodes, width
    )
    collected = []
    for part, plan in enumerate((RING_FIRST, PAIR_FIRST)):
        mine, theirs = results[part], results[2 + part]
        swapped = shift(theirs, "core", (2,), (1,))
        held, done = [], 0
        for slabs in plan:
            span = slice(done * nodes, (done + len(slabs)) * nodes)
            held.append(add(mine[span], swapped[span]).astype(BF16))
            done += len(slabs)
        scatter = scatter_ring_first if part == 0 else scatter_pair_first
        collected += scatter(held, row_axes)
    grad_features = final(collected, weight, PARTS)
    weight_sum = add(*around(weight_sum, "x", (4,), [(1,), (2,), (3,)]))
    weight_sum = add(*around(weight_sum, "core", (2,), [(1,)]))
    grad_weight = add(*around(weight_sum, ("zl", "zh"), (2, 2), [(0, 1), (1, 0), (1, 1)]))
    total_nodes = nodes * 128
    return activations, grad_features, grad_weight * float(total_nodes) ** -0.5


def solution(mesh):
    fine = Mesh(mesh.devices.reshape(2, 4, 2, 2, 4), ROW + COL)
    nodes = P(ROW + COL, None)
    return jax.shard_map(
        on_device,
        mesh=fine,
        in_specs=(
            nodes,
            P(),
            P(),
            P(ROW, COL, None, None, None),
            P(ROW, COL, None),
            P(ROW, COL, None),
            P(ROW, COL),
            nodes,
        ),
        out_specs=(nodes, nodes, P()),
        check_vma=False,
    )
```

```python
import functools

import jax
import jax.numpy as jnp
from jax import lax
from jax.experimental import pallas as pl
from jax.experimental.pallas import tpu as pltpu
from jax.sharding import Mesh
from jax.sharding import PartitionSpec as P

BF16 = jnp.bfloat16
F32 = jnp.float32
ROW = ("zl", "y", "core")
COL = ("zh", "x")
FORWARD_LIMIT = 40 * 2**20
BACKWARD_LIMIT = 48 * 2**20
SMALL_LIMIT = 14 * 2**20
PARTS = 2
BATCH = 48
CHUNK = 48


def accumulate(source_buf, tile_buf, total, src, dst, contract, batch, base):
    size = tile_buf.shape[1]
    products = []
    for lane in range(batch):
        start = pl.multiple_of(src[base + lane] * size, size)
        products.append(
            lax.dot_general(
                tile_buf[base + lane],
                source_buf[pl.ds(start, size), :],
                contract,
                preferred_element_type=F32,
            )
        )
    for lane in range(batch):
        span = pl.ds(pl.multiple_of(dst[base + lane] * size, size), size)
        total[span, :] = total[span, :] + products[lane]


def source_copies_of(sources, source_plan, source_buf, source_sems, slab):
    half = source_buf.shape[1] // PARTS
    copies = []
    for source, places in zip(sources, source_plan):
        for offset, place, number, part in places:
            copies.append(
                pltpu.make_async_copy(
                    source.at[pl.ds(offset * slab, number * slab)],
                    source_buf.at[pl.ds(place * slab, number * slab), pl.ds(part * half, half)],
                    source_sems.at[len(copies)],
                )
            )
    return copies


def forward_kernel(source_plan, result_plan, slab, batch, chunk, *refs):
    pieces, outputs = len(source_plan), len(result_plan)
    count, src, dst, tiles = refs[:4]
    sources = refs[4 : 4 + pieces]
    results = refs[4 + pieces : 4 + pieces + outputs]
    tile_buf, source_buf, total, stage, tile_sems, source_sems, result_sems = refs[4 + pieces + outputs :]
    live = count[0]
    chunks = (live + chunk - 1) // chunk

    def tile_copy(index):
        span = pl.ds(index * chunk, chunk)
        return pltpu.make_async_copy(tiles.at[span], tile_buf.at[span], tile_sems.at[index])

    source_copies = source_copies_of(sources, source_plan, source_buf, source_sems, slab)

    def start_tiles(index, carry):
        tile_copy(index).start()
        return carry

    start_tiles(0, 0)
    for copy in source_copies:
        copy.start()
    lax.fori_loop(1, chunks, start_tiles, 0)
    total[...] = jnp.zeros_like(total)
    for copy in source_copies:
        copy.wait()

    def on_chunk(index, carry):
        tile_copy(index).wait()

        def on_batch(step, inner):
            base = index * chunk + step * batch
            accumulate(
                source_buf, tile_buf, total, src, dst, (((1,), (0,)), ((), ())), batch, base
            )
            return inner

        steps = jnp.minimum(chunk // batch, (live - index * chunk + batch - 1) // batch)
        return lax.fori_loop(0, steps, on_batch, carry)

    lax.fori_loop(0, chunks, on_chunk, 0)
    copies = []
    for place in range(stage.shape[0] // slab):
        rows = slice(place * slab, (place + 1) * slab)
        stage[rows, :] = total[rows, :].astype(BF16)
        for result, (held, column) in zip(results, result_plan):
            if place in held:
                copy = pltpu.make_async_copy(
                    stage.at[pl.ds(place * slab, slab), pl.ds(column, result.shape[1])],
                    result.at[pl.ds(held.index(place) * slab, slab)],
                    result_sems.at[len(copies)],
                )
                copy.start()
                copies.append(copy)
    for copy in copies:
        copy.wait()


def forward_sweep(count, src, dst, tiles, sources, source_plan, result_plan, slab, width):
    slots, size, _ = tiles.shape
    part_width = width // PARTS
    source_slabs = max(p + n for places in source_plan for _, p, n, _ in places)
    source_copies = sum(len(places) for places in source_plan)
    result_slabs = max(max(slabs) for slabs, _ in result_plan) + 1
    copies = sum(len(slabs) for slabs, _ in result_plan)
    chunk = min(CHUNK, slots)
    batch = min(BATCH, chunk)
    any_spec = pl.BlockSpec(memory_space=pl.ANY)
    return pl.pallas_call(
        functools.partial(forward_kernel, source_plan, result_plan, slab, batch, chunk),
        grid_spec=pltpu.PrefetchScalarGridSpec(
            num_scalar_prefetch=3,
            grid=(1,),
            in_specs=[any_spec] * (1 + len(sources)),
            out_specs=[any_spec] * len(result_plan),
            scratch_shapes=[
                pltpu.VMEM(tiles.shape, BF16),
                pltpu.VMEM((source_slabs * slab, width), BF16),
                pltpu.VMEM((result_slabs * slab + size, width), F32),
                pltpu.VMEM((result_slabs * slab, width), BF16),
                pltpu.SemaphoreType.DMA((slots // chunk,)),
                pltpu.SemaphoreType.DMA((source_copies,)),
                pltpu.SemaphoreType.DMA((copies,)),
            ],
        ),
        out_shape=[
            jax.ShapeDtypeStruct((len(slabs) * slab, part_width), BF16) for slabs, _ in result_plan
        ],
        compiler_params=pltpu.CompilerParams(vmem_limit_bytes=FORWARD_LIMIT),
        cost_estimate=pl.CostEstimate(flops=1024, bytes_accessed=1024, transcendentals=0),
        name="forward",
    )(count, src, dst, tiles, *sources)


def backward_kernel(source_plan, slab, batch, chunk, *refs):
    pieces = len(source_plan)
    count, src, dst, slab_at, tiles = refs[:5]
    sources = refs[5 : 5 + pieces]
    results = refs[5 + pieces : 9 + pieces]
    tile_buf, source_buf, total, stage, tile_sems, source_sems, result_sems = refs[9 + pieces :]
    live = count[0]
    chunks = (live + chunk - 1) // chunk
    slabs = stage.shape[0] // slab
    per_slab = slab // tile_buf.shape[1]
    half = results[0].shape[1]

    def tile_copy(index):
        span = pl.ds(index * chunk, chunk)
        return pltpu.make_async_copy(tiles.at[span], tile_buf.at[span], tile_sems.at[index])

    source_copies = source_copies_of(sources, source_plan, source_buf, source_sems, slab)

    def start_tiles(index, carry):
        tile_copy(index).start()
        return carry

    start_tiles(0, 0)
    for copy in source_copies:
        copy.start()
    lax.fori_loop(1, chunks, start_tiles, 0)
    total[...] = jnp.zeros_like(total)
    for copy in source_copies:
        copy.wait()

    def result_copy(result, place, at, part):
        return pltpu.make_async_copy(
            stage.at[pl.ds(pl.multiple_of(place * slab, slab), slab), pl.ds(part * half, half)],
            result.at[pl.ds(pl.multiple_of(at * slab, slab), slab)],
            result_sems.at[place, part],
        )

    def flush(place, carry):
        rows = pl.ds(pl.multiple_of(place * slab, slab), slab)
        stage[rows, :] = total[rows, :].astype(BF16)
        offset = slab_at[place]
        at = offset % 8
        ring_at = (at % 4) * 2 + at // 4

        @pl.when(offset < 8)
        def _():
            result_copy(results[0], place, ring_at, 0).start()
            result_copy(results[1], place, at, 1).start()

        @pl.when(offset >= 8)
        def _():
            result_copy(results[2], place, ring_at, 0).start()
            result_copy(results[3], place, at, 1).start()

        return carry

    def on_chunk(index, flushed):
        tile_copy(index).wait()

        def on_batch(step, inner):
            base = index * chunk + step * batch
            accumulate(
                source_buf, tile_buf, total, src, dst, (((0,), (0,)), ((), ())), batch, base
            )
            return inner

        steps = jnp.minimum(chunk // batch, (live - index * chunk + batch - 1) // batch)
        lax.fori_loop(0, steps, on_batch, 0)
        last = jnp.minimum((index + 1) * chunk, live) - 1
        ready = jnp.where(index + 1 == chunks, slabs, dst[last] // per_slab)
        lax.fori_loop(flushed, ready, flush, 0)
        return ready

    lax.fori_loop(0, chunks, on_chunk, 0)
    for place in range(slabs):
        for part in range(2):
            result_copy(results[part], place, 0, part).wait()


def backward_sweep(count, src, dst, slab_at, tiles, sources, source_plan, slab, width):
    slots, size, _ = tiles.shape
    part_width = width // PARTS
    source_slabs = max(p + n for places in source_plan for _, p, n, _ in places)
    slabs = slab_at.shape[0]
    copies = sum(len(places) for places in source_plan)
    chunk = min(CHUNK, slots)
    batch = min(BATCH, chunk)
    any_spec = pl.BlockSpec(memory_space=pl.ANY)
    return pl.pallas_call(
        functools.partial(backward_kernel, source_plan, slab, batch, chunk),
        grid_spec=pltpu.PrefetchScalarGridSpec(
            num_scalar_prefetch=4,
            grid=(1,),
            in_specs=[any_spec] * (1 + len(sources)),
            out_specs=[any_spec] * 4,
            scratch_shapes=[
                pltpu.VMEM(tiles.shape, BF16),
                pltpu.VMEM((source_slabs * slab, width), BF16),
                pltpu.VMEM((slabs * slab + size, width), F32),
                pltpu.VMEM((slabs * slab, width), BF16),
                pltpu.SemaphoreType.DMA((slots // chunk,)),
                pltpu.SemaphoreType.DMA((copies,)),
                pltpu.SemaphoreType.DMA((slabs, 2)),
            ],
        ),
        out_shape=[jax.ShapeDtypeStruct((slabs // 2 * slab, part_width), BF16)] * 4,
        compiler_params=pltpu.CompilerParams(vmem_limit_bytes=BACKWARD_LIMIT),
        cost_estimate=pl.CostEstimate(flops=1024, bytes_accessed=1024, transcendentals=0),
        name="backward",
    )(count, src, dst, slab_at, tiles, *sources)


def split_dot(left, right, contract):
    high = left.astype(BF16)
    low = (left - high.astype(F32)).astype(BF16)
    first = lax.dot_general(high, right, contract, preferred_element_type=F32)
    return first + lax.dot_general(low, right, contract, preferred_element_type=F32)


def summed(refs, parts):
    per_part = len(refs) // parts
    columns = []
    for part in range(parts):
        group = refs[part * per_part : (part + 1) * per_part]
        value = group[0][...].astype(F32)
        for ref in group[1:]:
            value = value + ref[...].astype(F32)
        columns.append(value)
    return columns[0] if parts == 1 else jnp.concatenate(columns, axis=1)


def middle_kernel(parts, count, *refs):
    pieces = refs[:count]
    weight, bias, cotangent = refs[count : count + 3]
    act_ref = refs[count + 3]
    grads = refs[count + 4 : count + 4 + parts]
    weight_grad = refs[count + 4 + parts]
    gathered = summed(pieces, parts)
    shifted = split_dot(gathered, weight[...], (((1,), (0,)), ((), ()))) + bias[...]
    sig = 1.0 / (1.0 + jnp.exp(-shifted))
    act_ref[...] = (shifted * sig).astype(BF16)
    slope = sig * (1.0 + shifted * (1.0 - sig))
    grad = (cotangent[...].astype(F32) * slope).astype(BF16)
    width = grad.shape[1] // parts
    for part in range(parts):
        grads[part][...] = grad[:, part * width : (part + 1) * width]
    term = lax.dot_general(
        gathered.astype(BF16), grad, (((0,), (0,)), ((), ())), preferred_element_type=F32
    )

    @pl.when(pl.program_id(0) == 0)
    def _():
        weight_grad[...] = jnp.zeros_like(weight_grad)

    weight_grad[...] += term


def middle(pieces, weight, bias, cotangent, parts):
    rows, width = cotangent.shape
    steps = 2
    block = rows // steps
    part_spec = pl.BlockSpec((block, width // parts), lambda i: (i, 0))
    wide_spec = pl.BlockSpec((block, width), lambda i: (i, 0))
    whole = pl.BlockSpec((width, width), lambda i: (0, 0))
    return pl.pallas_call(
        functools.partial(middle_kernel, parts, len(pieces)),
        grid=(steps,),
        in_specs=[part_spec] * len(pieces) + [whole, pl.BlockSpec((1, width), lambda i: (0, 0)), wide_spec],
        out_specs=[wide_spec] + [part_spec] * parts + [whole],
        out_shape=[jax.ShapeDtypeStruct((rows, width), BF16)]
        + [jax.ShapeDtypeStruct((rows, width // parts), BF16)] * parts
        + [jax.ShapeDtypeStruct((width, width), F32)],
        compiler_params=pltpu.CompilerParams(vmem_limit_bytes=SMALL_LIMIT),
        name="middle",
    )(*pieces, weight, bias.reshape(1, width), cotangent)


def final_kernel(parts, count, *refs):
    weight, out = refs[count], refs[count + 1]
    grad = summed(refs[:count], parts).astype(BF16)
    out[...] = lax.dot_general(
        grad, weight[...], (((1,), (1,)), ((), ())), preferred_element_type=F32
    ).astype(BF16)


def final(pieces, weight, parts):
    rows = pieces[-1].shape[0]
    width = weight.shape[0]
    steps = 2
    block = rows // steps
    part_spec = pl.BlockSpec((block, width // parts), lambda i: (i, 0))
    return pl.pallas_call(
        functools.partial(final_kernel, parts, len(pieces)),
        grid=(steps,),
        in_specs=[part_spec] * len(pieces) + [pl.BlockSpec((width, width), lambda i: (0, 0))],
        out_specs=pl.BlockSpec((block, width), lambda i: (i, 0)),
        out_shape=jax.ShapeDtypeStruct((rows, width), BF16),
        compiler_params=pltpu.CompilerParams(vmem_limit_bytes=SMALL_LIMIT),
        name="final",
    )(*pieces, weight)


def shift(value, axes, sizes, offset):
    perm = []
    total = 1
    for size in sizes:
        total *= size
    for index in range(total):
        rest, coords = index, []
        for size in reversed(sizes):
            coords.append(rest % size)
            rest //= size
        coords.reverse()
        source = 0
        for coord, size, off in zip(coords, sizes, offset):
            source = source * size + (coord + off) % size
        perm.append((source, index))
    return lax.ppermute(value, axes, perm)


def add(*terms):
    return functools.reduce(lambda a, b: a + b, [term.astype(F32) for term in terms])


def toward(value, axes, dz, dr):
    return shift(value, axes, (2, 4), (dz, -dr))


def relay_kernel(*refs):
    ring, own, arrived = refs[:4], refs[4], refs[5]
    other, *terms = refs[6:]
    nodes = other.shape[0]
    total = ring[0][...].astype(F32)
    for piece in ring[1:]:
        total = total + piece[...].astype(F32)
    other[...] = total.astype(BF16)
    for index, term in enumerate(terms):
        span = slice((index + 1) * nodes, (index + 2) * nodes)
        term[...] = (own[span, :].astype(F32) + arrived[span, :].astype(F32)).astype(BF16)


def relay(ring, own, arrived):
    nodes, width = own.shape[0] // 4, own.shape[1]
    half = pl.BlockSpec((nodes, width), lambda i: (1, 0))
    whole = pl.BlockSpec(own.shape, lambda i: (0, 0))
    out = pl.BlockSpec((nodes, width), lambda i: (0, 0))
    return pl.pallas_call(
        relay_kernel,
        grid=(1,),
        in_specs=[half] * 4 + [whole] * 2,
        out_specs=[out] * 4,
        out_shape=[jax.ShapeDtypeStruct((nodes, width), BF16)] * 4,
        compiler_params=pltpu.CompilerParams(vmem_limit_bytes=SMALL_LIMIT),
        cost_estimate=pl.CostEstimate(flops=1024, bytes_accessed=1024, transcendentals=0),
        name="relay",
    )(*ring, own, arrived)


def scatter(held, axes):
    ring = [held[0]] + [toward(held[dr], axes, 0, dr) for dr in range(1, 4)]
    arrived = toward(held[5], axes, 1, 0)
    other, *terms = relay(ring, held[4], arrived)
    first = ring + [toward(other, axes, 1, 0)]
    return first + [held[4], arrived] + [toward(terms[dr - 1], axes, 0, dr) for dr in range(1, 4)]


def join_kernel(first, first_pair, *refs):
    ring = refs[:4]
    pair, both = refs[4:]
    nodes = first.shape[0]
    pair[:nodes, :] = first[...]
    pair[nodes:, :] = first_pair[...]
    for index, piece in enumerate(ring):
        both[index * nodes : (index + 1) * nodes, :] = piece[...]


def join(first, first_pair, ring):
    nodes, width = first.shape
    return pl.pallas_call(
        join_kernel,
        out_shape=[
            jax.ShapeDtypeStruct((2 * nodes, width), BF16),
            jax.ShapeDtypeStruct((4 * nodes, width), BF16),
        ],
        compiler_params=pltpu.CompilerParams(vmem_limit_bytes=SMALL_LIMIT),
        cost_estimate=pl.CostEstimate(flops=1024, bytes_accessed=1024, transcendentals=0),
        name="join",
    )(first, first_pair, *ring)


def around(value, axes, sizes, offsets):
    return [value] + [shift(value, axes, sizes, offset) for offset in offsets]


def gather(first, second, axes):
    ring_steps = [(0, 1), (0, 2), (0, 3)]
    first_pair = shift(first, axes, (2, 4), (1, 0))
    ring = around(second, axes, (2, 4), ring_steps)
    pair, both = join(first, first_pair, ring)
    later = [shift(pair, axes, (2, 4), step) for step in ring_steps]
    return [pair, both], later + [shift(both, axes, (2, 4), (1, 0))]


RING_FIRST = [[dr, 4 + dr] for dr in range(4)]
PAIR_FIRST = [[0, 1, 2, 3], [4, 5, 6, 7]]
GATHERED = [
    [(0, 0, 1, 0), (1, 4, 1, 0)],
    [(0, 0, 4, 1)],
    *[[(0, dr, 1, 0), (1, 4 + dr, 1, 0)] for dr in range(1, 4)],
    [(0, 4, 4, 1)],
]
OTHER_CORE = [[(at, held + 8, slabs, half) for at, held, slabs, half in places] for places in GATHERED]


def on_device(
    features, weight, layer_bias, tile_values, tile_rows, tile_cols, tile_count, cotangent
):
    tiles = tile_values[0, 0]
    slots, size, _ = tiles.shape
    nodes, width = features.shape
    per_slab = nodes // size
    count = tile_count.reshape(1)
    zl, y, core = (lax.axis_index(name) for name in ROW)
    zh, x = (lax.axis_index(name) for name in COL)
    part_width = width // PARTS
    row_axes, col_axes = ("zl", "y"), ("zh", "x")

    row_ids, col_ids = tile_rows[0, 0], tile_cols[0, 0]
    row_slab = row_ids // per_slab
    row_at = (((row_slab // 4) ^ zh) * 4 + (row_slab % 4 - x) % 4) * per_slab + row_ids % per_slab
    every = jnp.arange(16, dtype=jnp.int32)
    slab_at = (((every // 8) ^ zl) * 4 + (every // 2 % 4 - y) % 4) + ((every % 2) ^ core) * 8
    live = jnp.arange(slots, dtype=jnp.int32) < count[0]
    row_to = jnp.where(live, row_at, 8 * per_slab)
    col_slab = col_ids // per_slab
    col_from = (
        (((col_slab // 8) ^ zl) * 4 + (col_slab // 2 % 4 - y) % 4) + ((col_slab % 2) ^ core) * 8
    ) * per_slab + col_ids % per_slab
    col_to = jnp.where(live, col_ids, 16 * per_slab)

    early, later = gather(features[:, :part_width], features[:, part_width:], row_axes)
    others = [shift(piece, "core", (2,), (1,)) for piece in early + later]
    plan = [(slabs, 0) for slabs in RING_FIRST] + [(slabs, part_width) for slabs in PAIR_FIRST]
    held = forward_sweep(
        count, col_from, row_to, tiles, early + later + others, GATHERED + OTHER_CORE, plan, nodes, width
    )
    arrived = scatter(held, col_axes)
    activations, first, second, weight_term = middle(arrived, weight, layer_bias, cotangent, PARTS)

    early, later = gather(first, second, col_axes)
    weight_sum = add(*around(weight_term, row_axes, (2, 4), [(0, 1), (0, 2), (0, 3)]))
    results = backward_sweep(
        count, row_at, col_to, slab_at, tiles, early + later + [weight_sum], GATHERED + [[]], nodes, width
    )
    held = []
    for part, plan in enumerate((RING_FIRST, PAIR_FIRST)):
        mine, theirs = results[part], results[2 + part]
        swapped = shift(theirs, "core", (2,), (1,))
        done = 0
        for slabs in plan:
            span = slice(done * nodes, (done + len(slabs)) * nodes)
            held.append(add(mine[span], swapped[span]).astype(BF16))
            done += len(slabs)
    collected = scatter(held, row_axes)
    grad_features = final(collected, weight, PARTS)
    weight_sum = add(*around(weight_sum, "x", (4,), [(1,), (2,), (3,)]))
    weight_sum = add(*around(weight_sum, "core", (2,), [(1,)]))
    grad_weight = add(*around(weight_sum, ("zl", "zh"), (2, 2), [(0, 1), (1, 0), (1, 1)]))
    total_nodes = nodes * 128
    return activations, grad_features, grad_weight * float(total_nodes) ** -0.5


def solution(mesh):
    fine = Mesh(mesh.devices.reshape(2, 4, 2, 2, 4), ROW + COL)
    nodes = P(ROW + COL, None)
    return jax.shard_map(
        on_device,
        mesh=fine,
        in_specs=(
            nodes,
            P(),
            P(),
            P(ROW, COL, None, None, None),
            P(ROW, COL, None),
            P(ROW, COL, None),
            P(ROW, COL),
            nodes,
        ),
        out_specs=(nodes, nodes, P()),
        check_vma=False,
    )
```

```python
import functools

import jax
import jax.numpy as jnp
from jax import lax
from jax.experimental import pallas as pl
from jax.experimental.pallas import tpu as pltpu
from jax.sharding import Mesh
from jax.sharding import PartitionSpec as P

BF16 = jnp.bfloat16
F32 = jnp.float32
ROW = ("zl", "y", "core")
COL = ("zh", "x")
FORWARD_LIMIT = 40 * 2**20
BACKWARD_LIMIT = 48 * 2**20
SMALL_LIMIT = 14 * 2**20
PARTS = 2
BATCH = 48
CHUNK = 48


def accumulate(source_buf, tile_buf, total, src, dst, contract, batch, base):
    size = tile_buf.shape[1]
    products = []
    for lane in range(batch):
        start = pl.multiple_of(src[base + lane] * size, size)
        products.append(
            lax.dot_general(
                tile_buf[base + lane],
                source_buf[pl.ds(start, size), :],
                contract,
                preferred_element_type=F32,
            )
        )
    for lane in range(batch):
        span = pl.ds(pl.multiple_of(dst[base + lane] * size, size), size)
        total[span, :] = total[span, :] + products[lane]


def source_copies_of(sources, source_plan, source_buf, source_sems, slab):
    half = source_buf.shape[1] // PARTS
    copies = []
    for source, places in zip(sources, source_plan):
        for offset, place, number, part in places:
            copies.append(
                pltpu.make_async_copy(
                    source.at[pl.ds(offset * slab, number * slab)],
                    source_buf.at[pl.ds(place * slab, number * slab), pl.ds(part * half, half)],
                    source_sems.at[len(copies)],
                )
            )
    return copies


def forward_kernel(source_plan, result_plan, slab, batch, chunk, *refs):
    pieces, outputs = len(source_plan), len(result_plan)
    count, src, dst, tiles = refs[:4]
    sources = refs[4 : 4 + pieces]
    results = refs[4 + pieces : 4 + pieces + outputs]
    tile_buf, source_buf, total, stage, tile_sems, source_sems, result_sems = refs[4 + pieces + outputs :]
    live = count[0]
    chunks = (live + chunk - 1) // chunk

    def tile_copy(index):
        span = pl.ds(index * chunk, chunk)
        return pltpu.make_async_copy(tiles.at[span], tile_buf.at[span], tile_sems.at[index])

    source_copies = source_copies_of(sources, source_plan, source_buf, source_sems, slab)

    def start_tiles(index, carry):
        tile_copy(index).start()
        return carry

    start_tiles(0, 0)
    for copy in source_copies:
        copy.start()
    lax.fori_loop(1, chunks, start_tiles, 0)
    total[...] = jnp.zeros_like(total)
    for copy in source_copies:
        copy.wait()

    def on_chunk(index, carry):
        tile_copy(index).wait()

        def on_batch(step, inner):
            base = index * chunk + step * batch
            accumulate(
                source_buf, tile_buf, total, src, dst, (((1,), (0,)), ((), ())), batch, base
            )
            return inner

        steps = jnp.minimum(chunk // batch, (live - index * chunk + batch - 1) // batch)
        return lax.fori_loop(0, steps, on_batch, carry)

    lax.fori_loop(0, chunks, on_chunk, 0)
    copies = []
    for place in range(stage.shape[0] // slab):
        rows = slice(place * slab, (place + 1) * slab)
        stage[rows, :] = total[rows, :].astype(BF16)
        for result, (held, column) in zip(results, result_plan):
            if place in held:
                copy = pltpu.make_async_copy(
                    stage.at[pl.ds(place * slab, slab), pl.ds(column, result.shape[1])],
                    result.at[pl.ds(held.index(place) * slab, slab)],
                    result_sems.at[len(copies)],
                )
                copy.start()
                copies.append(copy)
    for copy in copies:
        copy.wait()


def forward_sweep(count, src, dst, tiles, sources, source_plan, result_plan, slab, width):
    slots, size, _ = tiles.shape
    part_width = width // PARTS
    source_slabs = max(p + n for places in source_plan for _, p, n, _ in places)
    source_copies = sum(len(places) for places in source_plan)
    result_slabs = max(max(slabs) for slabs, _ in result_plan) + 1
    copies = sum(len(slabs) for slabs, _ in result_plan)
    chunk = min(CHUNK, slots)
    batch = min(BATCH, chunk)
    any_spec = pl.BlockSpec(memory_space=pl.ANY)
    return pl.pallas_call(
        functools.partial(forward_kernel, source_plan, result_plan, slab, batch, chunk),
        grid_spec=pltpu.PrefetchScalarGridSpec(
            num_scalar_prefetch=3,
            grid=(1,),
            in_specs=[any_spec] * (1 + len(sources)),
            out_specs=[any_spec] * len(result_plan),
            scratch_shapes=[
                pltpu.VMEM(tiles.shape, BF16),
                pltpu.VMEM((source_slabs * slab, width), BF16),
                pltpu.VMEM((result_slabs * slab + size, width), F32),
                pltpu.VMEM((result_slabs * slab, width), BF16),
                pltpu.SemaphoreType.DMA((slots // chunk,)),
                pltpu.SemaphoreType.DMA((source_copies,)),
                pltpu.SemaphoreType.DMA((copies,)),
            ],
        ),
        out_shape=[
            jax.ShapeDtypeStruct((len(slabs) * slab, part_width), BF16) for slabs, _ in result_plan
        ],
        compiler_params=pltpu.CompilerParams(vmem_limit_bytes=FORWARD_LIMIT),
        cost_estimate=pl.CostEstimate(flops=1024, bytes_accessed=1024, transcendentals=0),
        name="forward",
    )(count, src, dst, tiles, *sources)


def backward_kernel(source_plan, slab, batch, chunk, *refs):
    pieces = len(source_plan)
    count, src, dst, slab_at, tiles = refs[:5]
    sources = refs[5 : 5 + pieces]
    results = refs[5 + pieces : 9 + pieces]
    tile_buf, source_buf, total, stage, tile_sems, source_sems, result_sems = refs[9 + pieces :]
    live = count[0]
    chunks = (live + chunk - 1) // chunk
    slabs = stage.shape[0] // slab
    per_slab = slab // tile_buf.shape[1]
    half = results[0].shape[1]

    def tile_copy(index):
        span = pl.ds(index * chunk, chunk)
        return pltpu.make_async_copy(tiles.at[span], tile_buf.at[span], tile_sems.at[index])

    source_copies = source_copies_of(sources, source_plan, source_buf, source_sems, slab)

    def start_tiles(index, carry):
        tile_copy(index).start()
        return carry

    start_tiles(0, 0)
    for copy in source_copies:
        copy.start()
    lax.fori_loop(1, chunks, start_tiles, 0)
    total[...] = jnp.zeros_like(total)
    for copy in source_copies:
        copy.wait()

    def result_copy(result, place, at, part):
        return pltpu.make_async_copy(
            stage.at[pl.ds(pl.multiple_of(place * slab, slab), slab), pl.ds(part * half, half)],
            result.at[pl.ds(pl.multiple_of(at * slab, slab), slab)],
            result_sems.at[place, part],
        )

    def flush(place, carry):
        rows = pl.ds(pl.multiple_of(place * slab, slab), slab)
        stage[rows, :] = total[rows, :].astype(BF16)
        offset = slab_at[place]
        at = offset % 8
        ring_at = (at % 4) * 2 + at // 4

        @pl.when(offset < 8)
        def _():
            result_copy(results[0], place, ring_at, 0).start()
            result_copy(results[1], place, at, 1).start()

        @pl.when(offset >= 8)
        def _():
            result_copy(results[2], place, ring_at, 0).start()
            result_copy(results[3], place, at, 1).start()

        return carry

    def on_chunk(index, flushed):
        tile_copy(index).wait()

        def on_batch(step, inner):
            base = index * chunk + step * batch
            accumulate(
                source_buf, tile_buf, total, src, dst, (((0,), (0,)), ((), ())), batch, base
            )
            return inner

        steps = jnp.minimum(chunk // batch, (live - index * chunk + batch - 1) // batch)
        lax.fori_loop(0, steps, on_batch, 0)
        last = jnp.minimum((index + 1) * chunk, live) - 1
        ready = jnp.where(index + 1 == chunks, slabs, dst[last] // per_slab)
        lax.fori_loop(flushed, ready, flush, 0)
        return ready

    lax.fori_loop(0, chunks, on_chunk, 0)
    for place in range(slabs):
        for part in range(2):
            result_copy(results[part], place, 0, part).wait()


def backward_sweep(count, src, dst, slab_at, tiles, sources, source_plan, slab, width):
    slots, size, _ = tiles.shape
    part_width = width // PARTS
    source_slabs = max(p + n for places in source_plan for _, p, n, _ in places)
    slabs = slab_at.shape[0]
    copies = sum(len(places) for places in source_plan)
    chunk = min(CHUNK, slots)
    batch = min(BATCH, chunk)
    any_spec = pl.BlockSpec(memory_space=pl.ANY)
    return pl.pallas_call(
        functools.partial(backward_kernel, source_plan, slab, batch, chunk),
        grid_spec=pltpu.PrefetchScalarGridSpec(
            num_scalar_prefetch=4,
            grid=(1,),
            in_specs=[any_spec] * (1 + len(sources)),
            out_specs=[any_spec] * 4,
            scratch_shapes=[
                pltpu.VMEM(tiles.shape, BF16),
                pltpu.VMEM((source_slabs * slab, width), BF16),
                pltpu.VMEM((slabs * slab + size, width), F32),
                pltpu.VMEM((slabs * slab, width), BF16),
                pltpu.SemaphoreType.DMA((slots // chunk,)),
                pltpu.SemaphoreType.DMA((copies,)),
                pltpu.SemaphoreType.DMA((slabs, 2)),
            ],
        ),
        out_shape=[jax.ShapeDtypeStruct((slabs // 2 * slab, part_width), BF16)] * 4,
        compiler_params=pltpu.CompilerParams(vmem_limit_bytes=BACKWARD_LIMIT),
        cost_estimate=pl.CostEstimate(flops=1024, bytes_accessed=1024, transcendentals=0),
        name="backward",
    )(count, src, dst, slab_at, tiles, *sources)


def split_dot(left, right, contract):
    high = left.astype(BF16)
    low = (left - high.astype(F32)).astype(BF16)
    first = lax.dot_general(high, right, contract, preferred_element_type=F32)
    return first + lax.dot_general(low, right, contract, preferred_element_type=F32)


def summed(refs, parts):
    per_part = len(refs) // parts
    columns = []
    for part in range(parts):
        group = refs[part * per_part : (part + 1) * per_part]
        value = group[0][...].astype(F32)
        for ref in group[1:]:
            value = value + ref[...].astype(F32)
        columns.append(value)
    return columns[0] if parts == 1 else jnp.concatenate(columns, axis=1)


def middle_kernel(parts, count, *refs):
    pieces = refs[:count]
    weight, bias, cotangent = refs[count : count + 3]
    act_ref = refs[count + 3]
    grads = refs[count + 4 : count + 4 + parts]
    weight_grad = refs[count + 4 + parts]
    gathered = summed(pieces, parts)
    shifted = split_dot(gathered, weight[...], (((1,), (0,)), ((), ()))) + bias[...]
    sig = 1.0 / (1.0 + jnp.exp(-shifted))
    act_ref[...] = (shifted * sig).astype(BF16)
    slope = sig * (1.0 + shifted * (1.0 - sig))
    grad = (cotangent[...].astype(F32) * slope).astype(BF16)
    width = grad.shape[1] // parts
    for part in range(parts):
        grads[part][...] = grad[:, part * width : (part + 1) * width]
    term = lax.dot_general(
        gathered.astype(BF16), grad, (((0,), (0,)), ((), ())), preferred_element_type=F32
    )

    @pl.when(pl.program_id(0) == 0)
    def _():
        weight_grad[...] = jnp.zeros_like(weight_grad)

    weight_grad[...] += term


def middle(pieces, weight, bias, cotangent, parts):
    rows, width = cotangent.shape
    steps = 2
    block = rows // steps
    part_spec = pl.BlockSpec((block, width // parts), lambda i: (i, 0))
    wide_spec = pl.BlockSpec((block, width), lambda i: (i, 0))
    whole = pl.BlockSpec((width, width), lambda i: (0, 0))
    return pl.pallas_call(
        functools.partial(middle_kernel, parts, len(pieces)),
        grid=(steps,),
        in_specs=[part_spec] * len(pieces) + [whole, pl.BlockSpec((1, width), lambda i: (0, 0)), wide_spec],
        out_specs=[wide_spec] + [part_spec] * parts + [whole],
        out_shape=[jax.ShapeDtypeStruct((rows, width), BF16)]
        + [jax.ShapeDtypeStruct((rows, width // parts), BF16)] * parts
        + [jax.ShapeDtypeStruct((width, width), F32)],
        compiler_params=pltpu.CompilerParams(vmem_limit_bytes=SMALL_LIMIT),
        name="middle",
    )(*pieces, weight, bias.reshape(1, width), cotangent)


def final_kernel(parts, count, *refs):
    weight, out = refs[count], refs[count + 1]
    grad = summed(refs[:count], parts).astype(BF16)
    out[...] = lax.dot_general(
        grad, weight[...], (((1,), (1,)), ((), ())), preferred_element_type=F32
    ).astype(BF16)


def final(pieces, weight, parts):
    rows = pieces[-1].shape[0]
    width = weight.shape[0]
    steps = 2
    block = rows // steps
    part_spec = pl.BlockSpec((block, width // parts), lambda i: (i, 0))
    return pl.pallas_call(
        functools.partial(final_kernel, parts, len(pieces)),
        grid=(steps,),
        in_specs=[part_spec] * len(pieces) + [pl.BlockSpec((width, width), lambda i: (0, 0))],
        out_specs=pl.BlockSpec((block, width), lambda i: (i, 0)),
        out_shape=jax.ShapeDtypeStruct((rows, width), BF16),
        compiler_params=pltpu.CompilerParams(vmem_limit_bytes=SMALL_LIMIT),
        name="final",
    )(*pieces, weight)


def shift(value, axes, sizes, offset):
    perm = []
    total = 1
    for size in sizes:
        total *= size
    for index in range(total):
        rest, coords = index, []
        for size in reversed(sizes):
            coords.append(rest % size)
            rest //= size
        coords.reverse()
        source = 0
        for coord, size, off in zip(coords, sizes, offset):
            source = source * size + (coord + off) % size
        perm.append((source, index))
    return lax.ppermute(value, axes, perm)


def exchange(value, axis, pairs):
    size = lax.axis_size(axis)
    perm = [(((((index + pairs) ^ 1) - pairs) % size), index) for index in range(size)]
    return lax.ppermute(value, axis, perm)


def add(*terms):
    return functools.reduce(lambda a, b: a + b, [term.astype(F32) for term in terms])


def toward(value, axes, dz, dr):
    return shift(value, axes, (2, 4), (dz, -dr))


def relay_kernel(*refs):
    ring, own, arrived = refs[:4], refs[4], refs[5]
    other, *terms = refs[6:]
    nodes = other.shape[0]
    total = ring[0][...].astype(F32)
    for piece in ring[1:]:
        total = total + piece[...].astype(F32)
    other[...] = total.astype(BF16)
    for index, term in enumerate(terms):
        span = slice((index + 1) * nodes, (index + 2) * nodes)
        term[...] = (own[span, :].astype(F32) + arrived[span, :].astype(F32)).astype(BF16)


def relay(ring, own, arrived):
    nodes, width = own.shape[0] // 4, own.shape[1]
    half = pl.BlockSpec((nodes, width), lambda i: (1, 0))
    whole = pl.BlockSpec(own.shape, lambda i: (0, 0))
    out = pl.BlockSpec((nodes, width), lambda i: (0, 0))
    return pl.pallas_call(
        relay_kernel,
        grid=(1,),
        in_specs=[half] * 4 + [whole] * 2,
        out_specs=[out] * 4,
        out_shape=[jax.ShapeDtypeStruct((nodes, width), BF16)] * 4,
        compiler_params=pltpu.CompilerParams(vmem_limit_bytes=SMALL_LIMIT),
        cost_estimate=pl.CostEstimate(flops=1024, bytes_accessed=1024, transcendentals=0),
        name="relay",
    )(*ring, own, arrived)


def scatter(held, axes):
    ring = [held[0]] + [toward(held[dr], axes, 0, dr) for dr in range(1, 4)]
    arrived = toward(held[5], axes, 1, 0)
    other, *terms = relay(ring, held[4], arrived)
    first = ring + [toward(other, axes, 1, 0)]
    return first + [held[4], arrived] + [toward(terms[dr - 1], axes, 0, dr) for dr in range(1, 4)]


def join_kernel(first, first_pair, *refs):
    ring = refs[:4]
    pair, both = refs[4:]
    nodes = first.shape[0]
    pair[:nodes, :] = first[...]
    pair[nodes:, :] = first_pair[...]
    for index, piece in enumerate(ring):
        both[index * nodes : (index + 1) * nodes, :] = piece[...]


def join(first, first_pair, ring):
    nodes, width = first.shape
    return pl.pallas_call(
        join_kernel,
        out_shape=[
            jax.ShapeDtypeStruct((2 * nodes, width), BF16),
            jax.ShapeDtypeStruct((4 * nodes, width), BF16),
        ],
        compiler_params=pltpu.CompilerParams(vmem_limit_bytes=SMALL_LIMIT),
        cost_estimate=pl.CostEstimate(flops=1024, bytes_accessed=1024, transcendentals=0),
        name="join",
    )(first, first_pair, *ring)


def around(value, axes, sizes, offsets):
    return [value] + [shift(value, axes, sizes, offset) for offset in offsets]


def gather(first, second, axes):
    ring_steps = [(0, 1), (0, 2), (0, 3)]
    first_pair = shift(first, axes, (2, 4), (1, 0))
    ring = around(second, axes, (2, 4), ring_steps)
    pair, both = join(first, first_pair, ring)
    later = [shift(pair, axes, (2, 4), step) for step in ring_steps]
    return [pair, both], later + [shift(both, axes, (2, 4), (1, 0))]


RING_FIRST = [[dr, 4 + dr] for dr in range(4)]
PAIR_FIRST = [[0, 1, 2, 3], [4, 5, 6, 7]]
GATHERED = [
    [(0, 0, 1, 0), (1, 4, 1, 0)],
    [(0, 0, 4, 1)],
    *[[(0, dr, 1, 0), (1, 4 + dr, 1, 0)] for dr in range(1, 4)],
    [(0, 4, 4, 1)],
]
OTHER_CORE = [[(at, held + 8, slabs, half) for at, held, slabs, half in places] for places in GATHERED]


def on_device(
    features, weight, layer_bias, tile_values, tile_rows, tile_cols, tile_count, cotangent
):
    tiles = tile_values[0, 0]
    slots, size, _ = tiles.shape
    nodes, width = features.shape
    per_slab = nodes // size
    count = tile_count.reshape(1)
    zl, y, core = (lax.axis_index(name) for name in ROW)
    zh, x = (lax.axis_index(name) for name in COL)
    part_width = width // PARTS
    row_axes, col_axes = ("zl", "y"), ("zh", "x")

    row_ids, col_ids = tile_rows[0, 0], tile_cols[0, 0]
    row_slab = row_ids // per_slab
    row_at = (((row_slab // 4) ^ zh) * 4 + (row_slab % 4 - x) % 4) * per_slab + row_ids % per_slab
    every = jnp.arange(16, dtype=jnp.int32)
    slab_at = (((every // 8) ^ zl) * 4 + (every // 2 % 4 - y) % 4) + ((every % 2) ^ core) * 8
    live = jnp.arange(slots, dtype=jnp.int32) < count[0]
    row_to = jnp.where(live, row_at, 8 * per_slab)
    col_slab = col_ids // per_slab
    col_from = (
        (((col_slab // 8) ^ zl) * 4 + (col_slab // 2 % 4 - y) % 4) + ((col_slab % 2) ^ core) * 8
    ) * per_slab + col_ids % per_slab
    col_to = jnp.where(live, col_ids, 16 * per_slab)

    early, later = gather(features[:, :part_width], features[:, part_width:], row_axes)
    others = [shift(piece, "core", (2,), (1,)) for piece in early + later]
    plan = [(slabs, 0) for slabs in RING_FIRST] + [(slabs, part_width) for slabs in PAIR_FIRST]
    held = forward_sweep(
        count, col_from, row_to, tiles, early + later + others, GATHERED + OTHER_CORE, plan, nodes, width
    )
    arrived = scatter(held, col_axes)
    activations, first, second, weight_term = middle(arrived, weight, layer_bias, cotangent, PARTS)

    early, later = gather(first, second, col_axes)
    weight_sum = weight_term + exchange(weight_term, "y", 0)
    weight_sum = weight_sum + exchange(weight_sum, "y", 1)
    results = backward_sweep(
        count, row_at, col_to, slab_at, tiles, early + later + [weight_sum], GATHERED + [[]], nodes, width
    )
    held = []
    for part, plan in enumerate((RING_FIRST, PAIR_FIRST)):
        mine, theirs = results[part], results[2 + part]
        swapped = shift(theirs, "core", (2,), (1,))
        done = 0
        for slabs in plan:
            span = slice(done * nodes, (done + len(slabs)) * nodes)
            held.append(add(mine[span], swapped[span]).astype(BF16))
            done += len(slabs)
    collected = scatter(held, row_axes)
    grad_features = final(collected, weight, PARTS)
    _, *others = around(weight_sum.astype(BF16), "x", (4,), [(1,), (2,), (3,)])
    weight_sum = add(weight_sum, *others)
    weight_sum = weight_sum + exchange(weight_sum, "core", 0)
    _, *others = around(weight_sum.astype(BF16), ("zl", "zh"), (2, 2), [(0, 1), (1, 0), (1, 1)])
    weight_sum = add(weight_sum, *others)
    total_nodes = nodes * 128
    return activations, grad_features, weight_sum * float(total_nodes) ** -0.5


def solution(mesh):
    fine = Mesh(mesh.devices.reshape(2, 4, 2, 2, 4), ROW + COL)
    nodes = P(ROW + COL, None)
    return jax.shard_map(
        on_device,
        mesh=fine,
        in_specs=(
            nodes,
            P(),
            P(),
            P(ROW, COL, None, None, None),
            P(ROW, COL, None),
            P(ROW, COL, None),
            P(ROW, COL),
            nodes,
        ),
        out_specs=(nodes, nodes, P()),
        check_vma=False,
    )
```

```python
import functools

import jax
import jax.numpy as jnp
from jax import lax
from jax.experimental import pallas as pl
from jax.experimental.pallas import tpu as pltpu
from jax.sharding import Mesh
from jax.sharding import PartitionSpec as P

BF16 = jnp.bfloat16
F32 = jnp.float32
ROW = ("zl", "y", "core")
COL = ("zh", "x")
FORWARD_LIMIT = 46 * 2**20
BACKWARD_LIMIT = 48 * 2**20
SMALL_LIMIT = 14 * 2**20
PARTS = 2
BATCH = 64
CHUNK = 64


def accumulate(source_buf, tile_buf, total, src, dst, contract, batch, base):
    size = tile_buf.shape[1]
    products = []
    for lane in range(batch):
        start = pl.multiple_of(src[base + lane] * size, size)
        products.append(
            lax.dot_general(
                tile_buf[base + lane],
                source_buf[pl.ds(start, size), :],
                contract,
                preferred_element_type=F32,
            )
        )
    for lane in range(batch):
        span = pl.ds(pl.multiple_of(dst[base + lane] * size, size), size)
        total[span, :] = total[span, :] + products[lane]


def source_copies_of(sources, source_plan, source_buf, source_sems, slab):
    half = source_buf.shape[1] // PARTS
    copies = []
    for source, places in zip(sources, source_plan):
        for offset, place, number, part in places:
            copies.append(
                pltpu.make_async_copy(
                    source.at[pl.ds(offset * slab, number * slab)],
                    source_buf.at[pl.ds(place * slab, number * slab), pl.ds(part * half, half)],
                    source_sems.at[len(copies)],
                )
            )
    return copies


def forward_kernel(source_plan, result_plan, slab, batch, chunk, *refs):
    pieces, outputs = len(source_plan), len(result_plan)
    count, src, dst, tiles = refs[:4]
    sources = refs[4 : 4 + pieces]
    results = refs[4 + pieces : 4 + pieces + outputs]
    tile_buf, source_buf, total, stage, tile_sems, source_sems, result_sems = refs[4 + pieces + outputs :]
    live = count[0]
    chunks = (live + chunk - 1) // chunk

    def tile_copy(index):
        span = pl.ds(index * chunk, chunk)
        return pltpu.make_async_copy(tiles.at[span], tile_buf.at[span], tile_sems.at[index])

    source_copies = source_copies_of(sources, source_plan, source_buf, source_sems, slab)

    def start_tiles(index, carry):
        tile_copy(index).start()
        return carry

    start_tiles(0, 0)
    for copy in source_copies:
        copy.start()
    lax.fori_loop(1, chunks, start_tiles, 0)
    total[...] = jnp.zeros_like(total)
    for copy in source_copies:
        copy.wait()

    def on_chunk(index, carry):
        tile_copy(index).wait()

        def on_batch(step, inner):
            base = index * chunk + step * batch
            accumulate(
                source_buf, tile_buf, total, src, dst, (((1,), (0,)), ((), ())), batch, base
            )
            return inner

        steps = jnp.minimum(chunk // batch, (live - index * chunk + batch - 1) // batch)
        return lax.fori_loop(0, steps, on_batch, carry)

    lax.fori_loop(0, chunks, on_chunk, 0)
    copies = []
    for place in range(stage.shape[0] // slab):
        rows = slice(place * slab, (place + 1) * slab)
        stage[rows, :] = total[rows, :].astype(BF16)
        for result, (held, column) in zip(results, result_plan):
            if place in held:
                copy = pltpu.make_async_copy(
                    stage.at[pl.ds(place * slab, slab), pl.ds(column, result.shape[1])],
                    result.at[pl.ds(held.index(place) * slab, slab)],
                    result_sems.at[len(copies)],
                )
                copy.start()
                copies.append(copy)
    for copy in copies:
        copy.wait()


def forward_sweep(count, src, dst, tiles, sources, source_plan, result_plan, slab, width):
    slots, size, _ = tiles.shape
    part_width = width // PARTS
    source_slabs = max(p + n for places in source_plan for _, p, n, _ in places)
    source_copies = sum(len(places) for places in source_plan)
    result_slabs = max(max(slabs) for slabs, _ in result_plan) + 1
    copies = sum(len(slabs) for slabs, _ in result_plan)
    chunk = min(CHUNK, slots)
    batch = min(BATCH, chunk)
    any_spec = pl.BlockSpec(memory_space=pl.ANY)
    return pl.pallas_call(
        functools.partial(forward_kernel, source_plan, result_plan, slab, batch, chunk),
        grid_spec=pltpu.PrefetchScalarGridSpec(
            num_scalar_prefetch=3,
            grid=(1,),
            in_specs=[any_spec] * (1 + len(sources)),
            out_specs=[any_spec] * len(result_plan),
            scratch_shapes=[
                pltpu.VMEM(tiles.shape, BF16),
                pltpu.VMEM((source_slabs * slab, width), BF16),
                pltpu.VMEM((result_slabs * slab + size, width), F32),
                pltpu.VMEM((result_slabs * slab, width), BF16),
                pltpu.SemaphoreType.DMA((slots // chunk,)),
                pltpu.SemaphoreType.DMA((source_copies,)),
                pltpu.SemaphoreType.DMA((copies,)),
            ],
        ),
        out_shape=[
            jax.ShapeDtypeStruct((len(slabs) * slab, part_width), BF16) for slabs, _ in result_plan
        ],
        compiler_params=pltpu.CompilerParams(vmem_limit_bytes=FORWARD_LIMIT),
        cost_estimate=pl.CostEstimate(flops=1024, bytes_accessed=1024, transcendentals=0),
        name="forward",
    )(count, src, dst, tiles, *sources)


def backward_kernel(source_plan, slab, batch, chunk, *refs):
    pieces = len(source_plan)
    count, src, dst, slab_at, tiles = refs[:5]
    sources = refs[5 : 5 + pieces]
    results = refs[5 + pieces : 9 + pieces]
    tile_buf, source_buf, total, stage, tile_sems, source_sems, result_sems = refs[9 + pieces :]
    live = count[0]
    chunks = (live + chunk - 1) // chunk
    slabs = stage.shape[0] // slab
    per_slab = slab // tile_buf.shape[1]
    half = results[0].shape[1]

    def tile_copy(index):
        span = pl.ds(index * chunk, chunk)
        return pltpu.make_async_copy(tiles.at[span], tile_buf.at[span], tile_sems.at[index])

    source_copies = source_copies_of(sources, source_plan, source_buf, source_sems, slab)

    def start_tiles(index, carry):
        tile_copy(index).start()
        return carry

    start_tiles(0, 0)
    for copy in source_copies:
        copy.start()
    lax.fori_loop(1, chunks, start_tiles, 0)
    total[...] = jnp.zeros_like(total)
    for copy in source_copies:
        copy.wait()

    def result_copy(result, place, at, part):
        return pltpu.make_async_copy(
            stage.at[pl.ds(pl.multiple_of(place * slab, slab), slab), pl.ds(part * half, half)],
            result.at[pl.ds(pl.multiple_of(at * slab, slab), slab)],
            result_sems.at[place, part],
        )

    def flush(place, carry):
        rows = pl.ds(pl.multiple_of(place * slab, slab), slab)
        stage[rows, :] = total[rows, :].astype(BF16)
        offset = slab_at[place]
        at = offset % 8
        ring_at = (at % 4) * 2 + at // 4

        @pl.when(offset < 8)
        def _():
            result_copy(results[0], place, ring_at, 0).start()
            result_copy(results[1], place, at, 1).start()

        @pl.when(offset >= 8)
        def _():
            result_copy(results[2], place, ring_at, 0).start()
            result_copy(results[3], place, at, 1).start()

        return carry

    def on_chunk(index, flushed):
        tile_copy(index).wait()

        def on_batch(step, inner):
            base = index * chunk + step * batch
            accumulate(
                source_buf, tile_buf, total, src, dst, (((0,), (0,)), ((), ())), batch, base
            )
            return inner

        steps = jnp.minimum(chunk // batch, (live - index * chunk + batch - 1) // batch)
        lax.fori_loop(0, steps, on_batch, 0)
        last = jnp.minimum((index + 1) * chunk, live) - 1
        ready = jnp.where(index + 1 == chunks, slabs, dst[last] // per_slab)
        lax.fori_loop(flushed, ready, flush, 0)
        return ready

    lax.fori_loop(0, chunks, on_chunk, 0)
    for place in range(slabs):
        for part in range(2):
            result_copy(results[part], place, 0, part).wait()


def backward_sweep(count, src, dst, slab_at, tiles, sources, source_plan, slab, width):
    slots, size, _ = tiles.shape
    part_width = width // PARTS
    source_slabs = max(p + n for places in source_plan for _, p, n, _ in places)
    slabs = slab_at.shape[0]
    copies = sum(len(places) for places in source_plan)
    chunk = min(CHUNK, slots)
    batch = min(BATCH, chunk)
    any_spec = pl.BlockSpec(memory_space=pl.ANY)
    return pl.pallas_call(
        functools.partial(backward_kernel, source_plan, slab, batch, chunk),
        grid_spec=pltpu.PrefetchScalarGridSpec(
            num_scalar_prefetch=4,
            grid=(1,),
            in_specs=[any_spec] * (1 + len(sources)),
            out_specs=[any_spec] * 4,
            scratch_shapes=[
                pltpu.VMEM(tiles.shape, BF16),
                pltpu.VMEM((source_slabs * slab, width), BF16),
                pltpu.VMEM((slabs * slab + size, width), F32),
                pltpu.VMEM((slabs * slab, width), BF16),
                pltpu.SemaphoreType.DMA((slots // chunk,)),
                pltpu.SemaphoreType.DMA((copies,)),
                pltpu.SemaphoreType.DMA((slabs, 2)),
            ],
        ),
        out_shape=[jax.ShapeDtypeStruct((slabs // 2 * slab, part_width), BF16)] * 4,
        compiler_params=pltpu.CompilerParams(vmem_limit_bytes=BACKWARD_LIMIT),
        cost_estimate=pl.CostEstimate(flops=1024, bytes_accessed=1024, transcendentals=0),
        name="backward",
    )(count, src, dst, slab_at, tiles, *sources)


def split_dot(left, right, contract):
    high = left.astype(BF16)
    low = (left - high.astype(F32)).astype(BF16)
    first = lax.dot_general(high, right, contract, preferred_element_type=F32)
    return first + lax.dot_general(low, right, contract, preferred_element_type=F32)


def summed(refs, parts):
    per_part = len(refs) // parts
    columns = []
    for part in range(parts):
        group = refs[part * per_part : (part + 1) * per_part]
        value = group[0][...].astype(F32)
        for ref in group[1:]:
            value = value + ref[...].astype(F32)
        columns.append(value)
    return columns[0] if parts == 1 else jnp.concatenate(columns, axis=1)


def middle_kernel(parts, count, *refs):
    pieces = refs[:count]
    weight, bias, cotangent = refs[count : count + 3]
    act_ref = refs[count + 3]
    grads = refs[count + 4 : count + 4 + parts]
    weight_grad = refs[count + 4 + parts]
    gathered = summed(pieces, parts)
    shifted = split_dot(gathered, weight[...], (((1,), (0,)), ((), ()))) + bias[...]
    sig = 1.0 / (1.0 + jnp.exp(-shifted))
    act_ref[...] = (shifted * sig).astype(BF16)
    slope = sig * (1.0 + shifted * (1.0 - sig))
    grad = (cotangent[...].astype(F32) * slope).astype(BF16)
    width = grad.shape[1] // parts
    for part in range(parts):
        grads[part][...] = grad[:, part * width : (part + 1) * width]
    term = lax.dot_general(
        gathered.astype(BF16), grad, (((0,), (0,)), ((), ())), preferred_element_type=F32
    )

    @pl.when(pl.program_id(0) == 0)
    def _():
        weight_grad[...] = jnp.zeros_like(weight_grad)

    weight_grad[...] += term


def middle(pieces, weight, bias, cotangent, parts):
    rows, width = cotangent.shape
    steps = 2
    block = rows // steps
    part_spec = pl.BlockSpec((block, width // parts), lambda i: (i, 0))
    wide_spec = pl.BlockSpec((block, width), lambda i: (i, 0))
    whole = pl.BlockSpec((width, width), lambda i: (0, 0))
    return pl.pallas_call(
        functools.partial(middle_kernel, parts, len(pieces)),
        grid=(steps,),
        in_specs=[part_spec] * len(pieces) + [whole, pl.BlockSpec((1, width), lambda i: (0, 0)), wide_spec],
        out_specs=[wide_spec] + [part_spec] * parts + [whole],
        out_shape=[jax.ShapeDtypeStruct((rows, width), BF16)]
        + [jax.ShapeDtypeStruct((rows, width // parts), BF16)] * parts
        + [jax.ShapeDtypeStruct((width, width), F32)],
        compiler_params=pltpu.CompilerParams(vmem_limit_bytes=SMALL_LIMIT),
        name="middle",
    )(*pieces, weight, bias.reshape(1, width), cotangent)


def final_kernel(parts, count, *refs):
    weight, out = refs[count], refs[count + 1]
    grad = summed(refs[:count], parts).astype(BF16)
    out[...] = lax.dot_general(
        grad, weight[...], (((1,), (1,)), ((), ())), preferred_element_type=F32
    ).astype(BF16)


def final(pieces, weight, parts):
    rows = pieces[-1].shape[0]
    width = weight.shape[0]
    steps = 2
    block = rows // steps
    part_spec = pl.BlockSpec((block, width // parts), lambda i: (i, 0))
    return pl.pallas_call(
        functools.partial(final_kernel, parts, len(pieces)),
        grid=(steps,),
        in_specs=[part_spec] * len(pieces) + [pl.BlockSpec((width, width), lambda i: (0, 0))],
        out_specs=pl.BlockSpec((block, width), lambda i: (i, 0)),
        out_shape=jax.ShapeDtypeStruct((rows, width), BF16),
        compiler_params=pltpu.CompilerParams(vmem_limit_bytes=SMALL_LIMIT),
        name="final",
    )(*pieces, weight)


def shift(value, axes, sizes, offset):
    perm = []
    total = 1
    for size in sizes:
        total *= size
    for index in range(total):
        rest, coords = index, []
        for size in reversed(sizes):
            coords.append(rest % size)
            rest //= size
        coords.reverse()
        source = 0
        for coord, size, off in zip(coords, sizes, offset):
            source = source * size + (coord + off) % size
        perm.append((source, index))
    return lax.ppermute(value, axes, perm)


def exchange(value, axis, pairs):
    size = lax.axis_size(axis)
    perm = [(((((index + pairs) ^ 1) - pairs) % size), index) for index in range(size)]
    return lax.ppermute(value, axis, perm)


def add(*terms):
    return functools.reduce(lambda a, b: a + b, [term.astype(F32) for term in terms])


def toward(value, axes, dz, dr):
    return shift(value, axes, (2, 4), (dz, -dr))


def relay_kernel(*refs):
    ring, own, arrived = refs[:4], refs[4], refs[5]
    other, *terms = refs[6:]
    nodes = other.shape[0]
    total = ring[0][...].astype(F32)
    for piece in ring[1:]:
        total = total + piece[...].astype(F32)
    other[...] = total.astype(BF16)
    for index, term in enumerate(terms):
        span = slice((index + 1) * nodes, (index + 2) * nodes)
        term[...] = (own[span, :].astype(F32) + arrived[span, :].astype(F32)).astype(BF16)


def relay(ring, own, arrived):
    nodes, width = own.shape[0] // 4, own.shape[1]
    half = pl.BlockSpec((nodes, width), lambda i: (1, 0))
    whole = pl.BlockSpec(own.shape, lambda i: (0, 0))
    out = pl.BlockSpec((nodes, width), lambda i: (0, 0))
    return pl.pallas_call(
        relay_kernel,
        grid=(1,),
        in_specs=[half] * 4 + [whole] * 2,
        out_specs=[out] * 4,
        out_shape=[jax.ShapeDtypeStruct((nodes, width), BF16)] * 4,
        compiler_params=pltpu.CompilerParams(vmem_limit_bytes=SMALL_LIMIT),
        cost_estimate=pl.CostEstimate(flops=1024, bytes_accessed=1024, transcendentals=0),
        name="relay",
    )(*ring, own, arrived)


def scatter(held, axes):
    ring = [held[0]] + [toward(held[dr], axes, 0, dr) for dr in range(1, 4)]
    arrived = toward(held[5], axes, 1, 0)
    other, *terms = relay(ring, held[4], arrived)
    first = ring + [toward(other, axes, 1, 0)]
    return first + [held[4], arrived] + [toward(terms[dr - 1], axes, 0, dr) for dr in range(1, 4)]


def join_kernel(first, first_pair, *refs):
    ring = refs[:4]
    pair, both = refs[4:]
    nodes = first.shape[0]
    pair[:nodes, :] = first[...]
    pair[nodes:, :] = first_pair[...]
    for index, piece in enumerate(ring):
        both[index * nodes : (index + 1) * nodes, :] = piece[...]


def join(first, first_pair, ring):
    nodes, width = first.shape
    return pl.pallas_call(
        join_kernel,
        out_shape=[
            jax.ShapeDtypeStruct((2 * nodes, width), BF16),
            jax.ShapeDtypeStruct((4 * nodes, width), BF16),
        ],
        compiler_params=pltpu.CompilerParams(vmem_limit_bytes=SMALL_LIMIT),
        cost_estimate=pl.CostEstimate(flops=1024, bytes_accessed=1024, transcendentals=0),
        name="join",
    )(first, first_pair, *ring)


def around(value, axes, sizes, offsets):
    return [value] + [shift(value, axes, sizes, offset) for offset in offsets]


def gather(first, second, axes):
    ring_steps = [(0, 1), (0, 2), (0, 3)]
    first_pair = shift(first, axes, (2, 4), (1, 0))
    ring = around(second, axes, (2, 4), ring_steps)
    pair, both = join(first, first_pair, ring)
    later = [shift(pair, axes, (2, 4), step) for step in ring_steps]
    return [pair, both], later + [shift(both, axes, (2, 4), (1, 0))]


RING_FIRST = [[dr, 4 + dr] for dr in range(4)]
PAIR_FIRST = [[0, 1, 2, 3], [4, 5, 6, 7]]
GATHERED = [
    [(0, 0, 1, 0), (1, 4, 1, 0)],
    [(0, 0, 4, 1)],
    *[[(0, dr, 1, 0), (1, 4 + dr, 1, 0)] for dr in range(1, 4)],
    [(0, 4, 4, 1)],
]
OTHER_CORE = [[(at, held + 8, slabs, half) for at, held, slabs, half in places] for places in GATHERED]


def on_device(
    features, weight, layer_bias, tile_values, tile_rows, tile_cols, tile_count, cotangent
):
    tiles = tile_values[0, 0]
    slots, size, _ = tiles.shape
    nodes, width = features.shape
    per_slab = nodes // size
    count = tile_count.reshape(1)
    zl, y, core = (lax.axis_index(name) for name in ROW)
    zh, x = (lax.axis_index(name) for name in COL)
    part_width = width // PARTS
    row_axes, col_axes = ("zl", "y"), ("zh", "x")

    row_ids, col_ids = tile_rows[0, 0], tile_cols[0, 0]
    row_slab = row_ids // per_slab
    row_at = (((row_slab // 4) ^ zh) * 4 + (row_slab % 4 - x) % 4) * per_slab + row_ids % per_slab
    every = jnp.arange(16, dtype=jnp.int32)
    slab_at = (((every // 8) ^ zl) * 4 + (every // 2 % 4 - y) % 4) + ((every % 2) ^ core) * 8
    live = jnp.arange(slots, dtype=jnp.int32) < count[0]
    row_to = jnp.where(live, row_at, 8 * per_slab)
    col_slab = col_ids // per_slab
    col_from = (
        (((col_slab // 8) ^ zl) * 4 + (col_slab // 2 % 4 - y) % 4) + ((col_slab % 2) ^ core) * 8
    ) * per_slab + col_ids % per_slab
    col_to = jnp.where(live, col_ids, 16 * per_slab)

    early, later = gather(features[:, :part_width], features[:, part_width:], row_axes)
    others = [shift(piece, "core", (2,), (1,)) for piece in early + later]
    plan = [(slabs, 0) for slabs in RING_FIRST] + [(slabs, part_width) for slabs in PAIR_FIRST]
    held = forward_sweep(
        count, col_from, row_to, tiles, early + later + others, GATHERED + OTHER_CORE, plan, nodes, width
    )
    arrived = scatter(held, col_axes)
    activations, first, second, weight_term = middle(arrived, weight, layer_bias, cotangent, PARTS)

    early, later = gather(first, second, col_axes)
    weight_sum = weight_term + exchange(weight_term, "y", 0)
    weight_sum = weight_sum + exchange(weight_sum, "y", 1)
    results = backward_sweep(
        count, row_at, col_to, slab_at, tiles, early + later + [weight_sum], GATHERED + [[]], nodes, width
    )
    held = []
    for part, plan in enumerate((RING_FIRST, PAIR_FIRST)):
        mine, theirs = results[part], results[2 + part]
        swapped = shift(theirs, "core", (2,), (1,))
        done = 0
        for slabs in plan:
            span = slice(done * nodes, (done + len(slabs)) * nodes)
            held.append(add(mine[span], swapped[span]).astype(BF16))
            done += len(slabs)
    collected = scatter(held, row_axes)
    grad_features = final(collected, weight, PARTS)
    _, *others = around(weight_sum.astype(BF16), "x", (4,), [(1,), (2,), (3,)])
    weight_sum = add(weight_sum, *others)
    weight_sum = weight_sum + exchange(weight_sum, "core", 0)
    _, *others = around(weight_sum.astype(BF16), ("zl", "zh"), (2, 2), [(0, 1), (1, 0), (1, 1)])
    weight_sum = add(weight_sum, *others)
    total_nodes = nodes * 128
    return activations, grad_features, weight_sum * float(total_nodes) ** -0.5


def solution(mesh):
    fine = Mesh(mesh.devices.reshape(2, 4, 2, 2, 4), ROW + COL)
    nodes = P(ROW + COL, None)
    return jax.shard_map(
        on_device,
        mesh=fine,
        in_specs=(
            nodes,
            P(),
            P(),
            P(ROW, COL, None, None, None),
            P(ROW, COL, None),
            P(ROW, COL, None),
            P(ROW, COL),
            nodes,
        ),
        out_specs=(nodes, nodes, P()),
        check_vma=False,
    )
```
